256 devices in a mesh: fsdp: 64 (over z, x, core), tp: 4 (over y).
Axes of the slice: x: 4, y: 4, z: 8, core: 2. Of those that a mesh axis runs over, the one named last changes fastest.
Arguments:
- weight: float32 [2, 8192, 8192], P(None, 'fsdp', 'tp'), may hold values from -6 to 6
- gradient: bfloat16 [2, 8192, 8192], P(None, 'fsdp', 'tp'), may hold values from -6 to 6
- momentum: float32 [2, 8192, 8192], P(None, 'fsdp', 'tp'), may hold values from -24 to 24
- right_basis: bfloat16 [2, 8192, 128], P(None, 'tp'), may hold values from -4 to 4
Outputs:
- new_weight: float32 [2, 8192, 8192], P(None, 'fsdp', 'tp')
- new_momentum: float32 [2, 8192, 8192], P(None, 'fsdp', 'tp')
- new_basis: bfloat16 [2, 8192, 128], P(None, 'tp')
The draws below stay inside these ranges and needn't reach their ends.
All inputs are finite; a program needn't handle non-finite values.
Results may differ from the reference program's by a relative error of at most 0.001.
Values sent between devices are 32-bit elements; how exact they have to be, the bound alone decides.
No kernel may reach another device: no remote copies, remote signals or barrier semaphores. Data moves between devices by JAX's collectives and lax.ppermute only.
A program may use at most 64 MiB of HBM per device.

```python
import math
import jax
import jax.numpy as jnp
from jax import lax

D = 8192
R = 128
LAYERS = 2


def draw_momentum(key, part):
    key = jax.random.fold_in(key, 11)
    position = jnp.arange(D, dtype=jnp.float32).reshape(1, D, 1) / (D - 1)
    values = jnp.clip(jax.random.normal(key, (LAYERS, D, D), jnp.float32), -4.0, 4.0)
    growth = jnp.exp(math.log(6.0) * position)
    return values * growth


def block_scale(rng, dims, split, smallest, largest):
    factor_of, own = 1.0, jax.random.fold_in(rng, 6)
    for dim, shards_of in split:
        draws = jnp.exp(jax.random.uniform(jax.random.fold_in(own, dim), (shards_of,), jnp.float32, smallest / len(split), largest / len(split)))
        factor_of = factor_of * jnp.repeat(draws, dims[dim] // shards_of).reshape([-1 if axis == dim else 1 for axis in range(len(dims))])
    return factor_of


def gaussian(rng, extent, scale, bound, split=(), kind=jnp.bfloat16):
    entries = scale * jax.random.normal(rng, extent, jnp.float32)
    if split:
        entries = entries * block_scale(rng, extent, split, -0.22, 0.18)
    return jnp.clip(entries, -bound, bound).astype(kind)


def setup_inputs(seed: int = 0) -> dict:
    arg_keys = jax.random.split(jax.random.key(seed), 5)
    weight = gaussian(arg_keys[0], (LAYERS, D, D), 1.0, 6.0, ((1, 64), (2, 4)), jnp.float32)
    gradient = gaussian(arg_keys[1], (LAYERS, D, D), 1.0, 6.0, ((1, 64), (2, 4)))
    momentum = draw_momentum(jax.random.fold_in(arg_keys[4], 71), 0)
    right_basis = gaussian(arg_keys[3], (LAYERS, D, R), 1.0, 4.0, ((1, 4),))
    return dict(weight=weight, gradient=gradient, momentum=momentum, right_basis=right_basis)


HIGH = lax.Precision.HIGHEST

def orthonormal(panel):
    gram = jnp.dot(panel.T, panel, precision=HIGH)
    factor_low = jnp.linalg.cholesky(gram)
    return jax.scipy.linalg.solve_triangular(factor_low, panel.T, lower=True).T

def reference(weight, gradient, momentum, right_basis):
    weights_out = []
    moments_out = []
    bases_out = []
    for layer_idx in range(LAYERS):
        buffer = momentum[layer_idx] + gradient[layer_idx].astype(jnp.float32)
        panel = jnp.dot(buffer, right_basis[layer_idx].astype(jnp.float32), precision=HIGH)
        basis_left = orthonormal(panel)
        reduced = jnp.dot(buffer.T, basis_left, precision=HIGH)
        column = reduced / jnp.sqrt(lax.optimization_barrier(jnp.sum(reduced * reduced, axis=0)) / D + 1e-06)
        moments_out.append(buffer - 0.05 * jnp.dot(basis_left, reduced.T, precision=HIGH))
        update = jnp.dot(basis_left, column.T, precision=HIGH) * math.sqrt(D / R)
        weights_out.append((1.0 - 0.05 * 0.1) * weight[layer_idx] - 0.05 * update)
        bases_out.append(column.astype(jnp.bfloat16))
    return (jnp.stack(weights_out), jnp.stack(moments_out), jnp.stack(bases_out))
```

```python
import math

import jax
import jax.numpy as jnp
from jax import lax
from jax.experimental import pallas as pl
from jax.experimental.pallas import tpu as pltpu
from jax.sharding import PartitionSpec as P

D = 8192
R = 128
LAYERS = 2
ROWS = 128
COLS = 2048
PIECE = 256
BAND = 16
BLOCK = 8

HIGHEST = lax.Precision.HIGHEST
F32 = jnp.float32
BF16 = jnp.bfloat16

VM = pl.BlockSpec(memory_space=pltpu.VMEM)
SM = pl.BlockSpec(memory_space=pltpu.SMEM)
ANY = pl.BlockSpec(memory_space=pl.ANY)
PARAMS = pltpu.CompilerParams(vmem_limit_bytes=40 << 20)


def struct(*shape, dtype=F32):
    return jax.ShapeDtypeStruct(shape, dtype)


def call(kernel, outs, ins, args, flops=1 << 20, nbytes=1 << 20, scratch=(), out_specs=None):
    return pl.pallas_call(
        kernel,
        out_shape=outs,
        in_specs=ins,
        out_specs=out_specs or jax.tree.map(lambda _: VM, outs),
        scratch_shapes=list(scratch),
        compiler_params=PARAMS,
        cost_estimate=pl.CostEstimate(flops=flops, bytes_accessed=nbytes, transcendentals=0),
    )(*args)


def split2(a):
    high = a.astype(BF16)
    return high, (a - high.astype(F32)).astype(BF16)


def split3(a):
    high = a.astype(BF16)
    rest = a - high.astype(F32)
    mid = rest.astype(BF16)
    return high, mid, (rest - mid.astype(F32)).astype(BF16)


def dot(a, b, dims):
    return lax.dot_general(a, b, (dims, ((), ())), preferred_element_type=F32)


def dot_x3(a, b, dims):
    ah, al = split2(a)
    bh, bl = split2(b)
    return dot(ah, bh, dims) + (dot(ah, bl, dims) + dot(al, bh, dims))


def panel_kernel(momentum, gradient, right, out, mom_v, grad_v, right_v, sems):
    pieces = 2
    width = COLS // pieces
    copies = []
    for layer in range(LAYERS):
        for piece in range(pieces):
            cut = slice(piece * width, (piece + 1) * width)
            slot = len(copies)
            group = [
                pltpu.make_async_copy(momentum.at[layer, :, cut], mom_v.at[layer, :, cut], sems.at[slot, 0]),
                pltpu.make_async_copy(gradient.at[layer, :, cut], grad_v.at[layer, :, cut], sems.at[slot, 1]),
                pltpu.make_async_copy(right.at[layer, cut, :], right_v.at[layer, cut, :], sems.at[slot, 2]),
            ]
            for item in group:
                item.start()
            copies.append(group)
    for layer in range(LAYERS):
        total = jnp.zeros((ROWS, R), F32)
        for piece in range(pieces):
            for item in copies[layer * pieces + piece]:
                item.wait()
            cut = slice(piece * width, (piece + 1) * width)
            buffer = mom_v[layer, :, cut] + grad_v[layer, :, cut].astype(F32)
            factor = right_v[layer, cut, :]
            high, mid, low = split3(buffer)
            dims = ((1,), (0,))
            total += dot(high, factor, dims) + (dot(mid, factor, dims) + dot(low, factor, dims))
        out[layer] = total


def gram_kernel(ids, p0, p1, p2, p3, panel, quarter):
    tp = ids[4]
    for layer in range(LAYERS):
        whole = (p0[layer] + p1[layer]) + (p2[layer] + p3[layer])
        panel[layer] = whole
        gram = lax.dot_general(whole, whole, (((0,), (0,)), ((), ())), precision=HIGHEST, preferred_element_type=F32)
        part = jnp.zeros((R // 4, R), F32)
        for pick in range(4):
            part = jnp.where(tp == pick, gram[pick * 32 : pick * 32 + 32], part)
        quarter[layer] = part


def product_kernel(flip, ids, panel, momentum, gradient, out):
    core = ids[0]
    x = ids[1]
    if flip:
        core = 1 - core
    for layer in range(LAYERS):
        panel_t = panel[layer].T
        for step in range(4):
            start = pl.multiple_of((core * 4 + lax.rem(x + step, 4)) * PIECE, PIECE)
            buffer = momentum[layer, :, pl.ds(start, PIECE)] + gradient[layer, :, pl.ds(start, PIECE)].astype(F32)
            out[step, layer] = dot_x3(panel_t, buffer, ((1,), (0,)))


def sum_x_kernel(ids, s0, r1, r2, r3, send, keep):
    low, high = ids[2], ids[3]
    for layer in range(LAYERS):
        for step in range(4):
            band = lax.rem(high + step, 4) * 2
            for out, bit in ((send, 1 - low), (keep, low)):
                rows = pl.ds(pl.multiple_of((band + bit) * BAND, BAND), BAND)
                out[step, layer] = (s0[layer, rows, :] + r1[layer, rows, :]) + (r2[layer, rows, :] + r3[layer, rows, :])


def cholesky_kernel(ids, q0, q1, q2, q3, out, work):
    tp = ids[4]
    for step, quarter in enumerate((q0, q1, q2, q3)):
        start = pl.multiple_of(lax.rem(tp + 4 - step, 4) * 32, 32)
        for layer in range(LAYERS):
            work[layer, pl.ds(start, 32), 0:R] = quarter[layer]
    rows_id = lax.broadcasted_iota(jnp.int32, (R, R), 0)
    cols_id = lax.broadcasted_iota(jnp.int32, (R, R), 1)
    unit = jnp.where(rows_id == cols_id, 1.0, 0.0).astype(F32)
    for layer in range(LAYERS):
        work[layer, :, R : 2 * R] = unit
    for base in range(0, R, BLOCK):
        for layer in range(LAYERS):
            rows = [work[layer, base + i : base + i + 1, :] for i in range(BLOCK)]
            square = [
                [jnp.broadcast_to(rows[i][:, base + j : base + j + 1], (1, 2 * R)) for j in range(i + 1)] for i in range(BLOCK)
            ]
            for j in range(BLOCK):
                pivot = square[j][j]
                inverse = lax.rsqrt(pivot)
                inverse = inverse * (1.5 - 0.5 * pivot * inverse * inverse)
                rows[j] = rows[j] * inverse
                for i in range(j + 1, BLOCK):
                    square[i][j] = square[i][j] * inverse
                for i in range(j + 1, BLOCK):
                    for k in range(j + 1, i + 1):
                        square[i][k] = square[i][k] - square[i][j] * square[k][j]
                    rows[i] = rows[i] - square[i][j] * rows[j]
            done = jnp.concatenate(rows, axis=0)
            out[layer, base : base + BLOCK, :] = done[:, R:]
            after = base + BLOCK
            if after < R:
                left = done[:, 0:R]
                lh, lm, ll = split3(left)
                dh, dm, dl = split3(done)
                stack_l = jnp.concatenate([lh, lm, lh, lm, ll, lh], axis=0)
                stack_d = jnp.concatenate([dh, dh, dm, dm, dh, dl], axis=0)
                change = dot(stack_l, stack_d, ((0,), (0,)))
                work[layer, after:, :] = work[layer, after:, :] - change[after:, :]


def spread_kernel(ids, inverse, m0, m1, m2, m3, o0, o1, o2, o3, out, squares, whole):
    low, high = ids[2], ids[3]
    for bit, group in ((low, (m0, m1, m2, m3)), (1 - low, (o0, o1, o2, o3))):
        for step in range(4):
            band = lax.rem(high + 4 - step, 4) * 2 + bit
            rows = pl.ds(pl.multiple_of(band * BAND, BAND), BAND)
            for layer in range(LAYERS):
                whole[layer, rows, :] = group[step][layer]
    ones = jnp.ones((8, PIECE), F32)
    for layer in range(LAYERS):
        reduced = lax.dot_general(
            inverse[layer], whole[layer], (((1,), (0,)), ((), ())), precision=HIGHEST, preferred_element_type=F32
        )
        out[layer] = reduced
        squares[layer] = lax.dot_general(
            ones, reduced * reduced, (((1,), (1,)), ((), ())), precision=HIGHEST, preferred_element_type=F32
        )


def final_kernel(
    ids, panel, inverse, squares, a0, a1, a2, a3, b0, b1, b2, b3, weight, momentum, gradient,
    new_weight, new_momentum, new_basis, weight_v, momentum_v, basis_v, sems,
):
    core, x = ids[0], ids[1]
    copies = []
    for layer in range(LAYERS):
        left = lax.dot_general(
            panel[layer], inverse[layer], (((1,), (1,)), ((), ())), precision=HIGHEST, preferred_element_type=F32
        )
        scale = lax.rsqrt(squares[layer, 0:1, :] * (1.0 / D) + 1e-06)
        both = jnp.concatenate([left * 0.05, left * (scale * (0.05 * math.sqrt(D / R)))], axis=0)
        for own, group in ((core, (a0, a1, a2, a3)), (1 - core, (b0, b1, b2, b3))):
            for step in range(4):
                start = pl.multiple_of((own * 4 + lax.rem(x + 4 - step, 4)) * PIECE, PIECE)
                cut = pl.ds(start, PIECE)
                reduced = group[step][layer]
                change = dot_x3(both, reduced, ((1,), (0,)))
                momentum_v[layer, :, cut] = (
                    momentum[layer, :, cut] + gradient[layer, :, cut].astype(F32)
                ) - change[0:ROWS]
                weight_v[layer, :, cut] = (1.0 - 0.05 * 0.1) * weight[layer, :, cut] - change[ROWS:]
                basis_v[layer, cut, :] = (reduced.T * scale).astype(BF16)
                slot = len(copies)
                group_copies = [
                    pltpu.make_async_copy(momentum_v.at[layer, :, cut], new_momentum.at[layer, :, cut], sems.at[slot, 0]),
                    pltpu.make_async_copy(weight_v.at[layer, :, cut], new_weight.at[layer, :, cut], sems.at[slot, 1]),
                    pltpu.make_async_copy(basis_v.at[layer, cut, :], new_basis.at[layer, cut, :], sems.at[slot, 2]),
                ]
                for item in group_copies:
                    item.start()
                copies.append(group_copies)
    for group_copies in copies:
        for item in group_copies:
            item.wait()


def place(z, x, core):
    return (z * 4 + x) * 2 + core


def fsdp_moves(dz, dx, flip_core=0, flip_z=0):
    return [
        (place(z, x, c), place(((z ^ flip_z) + dz) % 8, (x + dx) % 4, c ^ flip_core))
        for z in range(8)
        for x in range(4)
        for c in range(2)
    ]


def move_core(a):
    return lax.ppermute(a, "fsdp", fsdp_moves(0, 0, flip_core=1))


def move_x(a, step):
    return lax.ppermute(a, "fsdp", fsdp_moves(0, step))


def move_z(a, step):
    return lax.ppermute(a, "fsdp", fsdp_moves(step, 0))


def move_pair(a, flip_core=0):
    return lax.ppermute(a, "fsdp", fsdp_moves(0, 0, flip_core, 1))


def move_tp(a, step):
    return lax.ppermute(a, "tp", [(i, (i + step) % 4) for i in range(4)])


def body(weight, gradient, momentum, right_basis):
    index = lax.axis_index("fsdp")
    z = index // 8
    ids = jnp.stack([index % 2, (index // 2) % 4, z % 2, z // 2, lax.axis_index("tp")]).astype(jnp.int32)

    with jax.named_scope("panel"):
        part = call(
            panel_kernel, struct(LAYERS, ROWS, R), [ANY] * 3, (momentum, gradient, right_basis), 300 << 20, 4 << 20,
            scratch=[
                pltpu.VMEM((LAYERS, ROWS, COLS), F32), pltpu.VMEM((LAYERS, ROWS, COLS), BF16),
                pltpu.VMEM((LAYERS, COLS, R), BF16), pltpu.SemaphoreType.DMA((4, 3)),
            ],
        )
        parts = [move_tp(part, step) for step in (1, 2, 3)]
    with jax.named_scope("gram"):
        panel, quarter = call(
            gram_kernel, (struct(LAYERS, ROWS, R), struct(LAYERS, R // 4, R)), [SM] + [VM] * 4, (ids, part, *parts)
        )
        quarter = quarter + ((move_core(quarter) + move_pair(quarter)) + move_pair(quarter, 1))
        quarter = quarter + ((move_x(quarter, 1) + move_x(quarter, 3)) + move_x(quarter, 2))
        quarter = quarter + ((move_z(quarter, 2) + move_z(quarter, 6)) + move_z(quarter, 4))
        inverse = call(
            cholesky_kernel, struct(LAYERS, R, R), [SM] + [VM] * 4,
            (ids, quarter, *[move_tp(quarter, step) for step in (1, 2, 3)]),
            scratch=[pltpu.VMEM((LAYERS, R, 2 * R), F32)],
        )
    with jax.named_scope("product"):
        send, keep = [
            call(
                lambda *refs, flip=flip: product_kernel(flip, *refs), struct(4, LAYERS, R, PIECE),
                [SM] + [VM] * 3, (ids, panel, momentum, gradient), 300 << 20, 3 << 20,
            )
            for flip in (True, False)
        ]
        got = move_core(send)
        sums = [keep[step] + got[step] for step in range(4)]
    with jax.named_scope("scatter"):
        arrived = [move_x(sums[step], step) for step in (1, 2, 3)]
        z_send, z_keep = call(
            sum_x_kernel, (struct(4, LAYERS, BAND, PIECE),) * 2, [SM] + [VM] * 4, (ids, sums[0], *arrived)
        )
        z_got = move_pair(z_send)
        bands = [z_keep[step] + z_got[step] for step in range(4)]
        own = bands[0] + ((move_z(bands[1], 2) + move_z(bands[3], 6)) + move_z(bands[2], 4))
    with jax.named_scope("gather"):
        mine = [own] + [move_z(own, 2 * step) for step in (1, 2, 3)]
        others = move_pair(jnp.stack(mine))
        reduced, squares = call(
            spread_kernel, (struct(LAYERS, R, PIECE), struct(LAYERS, 8, R)), [SM] + [VM] * 9,
            (ids, inverse, *mine, *[others[step] for step in range(4)]),
            scratch=[pltpu.VMEM((LAYERS, R, PIECE), F32)],
        )
        group = [reduced] + [move_x(reduced, step) for step in (1, 2, 3)]
        across = [move_core(item) for item in group]
        squares = squares + ((move_tp(squares, 1) + move_tp(squares, 3)) + move_tp(squares, 2))
        squares = squares + ((move_x(squares, 1) + move_x(squares, 3)) + move_x(squares, 2))
        squares = squares + move_core(squares)
    with jax.named_scope("update"):
        return call(
            final_kernel,
            (
                struct(LAYERS, ROWS, COLS), struct(LAYERS, ROWS, COLS), struct(LAYERS, COLS, R, dtype=BF16),
            ),
            [SM] + [VM] * 14,
            (ids, panel, inverse, squares, *group, *across, weight, momentum, gradient),
            800 << 20, 11 << 20,
            scratch=[
                pltpu.VMEM((LAYERS, ROWS, COLS), F32), pltpu.VMEM((LAYERS, ROWS, COLS), F32),
                pltpu.VMEM((LAYERS, COLS, R), BF16), pltpu.SemaphoreType.DMA((16, 3)),
            ],
            out_specs=(ANY,) * 3,
        )


def solution(mesh):
    return jax.shard_map(
        body,
        mesh=mesh,
        in_specs=(
            P(None, "fsdp", "tp"),
            P(None, "fsdp", "tp"),
            P(None, "fsdp", "tp"),
            P(None, "tp", None),
        ),
        out_specs=(P(None, "fsdp", "tp"), P(None, "fsdp", "tp"), P(None, "tp", None)),
        check_vma=False,
    )
```

```python
import math

import jax
import jax.numpy as jnp
from jax import lax
from jax.experimental import pallas as pl
from jax.experimental.pallas import tpu as pltpu
from jax.sharding import PartitionSpec as P

D = 8192
R = 128
LAYERS = 2
ROWS = 128
COLS = 2048
PIECE = 256
BAND = 16
GRAM = 8
BLOCK = 8

HIGHEST = lax.Precision.HIGHEST
F32 = jnp.float32
BF16 = jnp.bfloat16

VM = pl.BlockSpec(memory_space=pltpu.VMEM)
SM = pl.BlockSpec(memory_space=pltpu.SMEM)
ANY = pl.BlockSpec(memory_space=pl.ANY)
HBM = pl.BlockSpec(memory_space=pltpu.HBM)


def struct(*shape, dtype=F32):
    return jax.ShapeDtypeStruct(shape, dtype)


def call(kernel, outs, ins, args, flops=1 << 20, nbytes=1 << 20, scratch=(), out_specs=None, limit=16 << 20):
    return pl.pallas_call(
        kernel,
        out_shape=outs,
        in_specs=ins,
        out_specs=out_specs or jax.tree.map(lambda _: VM, outs),
        scratch_shapes=list(scratch),
        compiler_params=pltpu.CompilerParams(vmem_limit_bytes=limit),
        cost_estimate=pl.CostEstimate(flops=flops, bytes_accessed=nbytes, transcendentals=0),
    )(*args)


def split2(a):
    high = a.astype(BF16)
    return high, (a - high.astype(F32)).astype(BF16)


def split3(a):
    high = a.astype(BF16)
    rest = a - high.astype(F32)
    mid = rest.astype(BF16)
    return high, mid, (rest - mid.astype(F32)).astype(BF16)


def dot(a, b, dims):
    return lax.dot_general(a, b, (dims, ((), ())), preferred_element_type=F32)


def dot_x3(a, b, dims):
    ah, al = split2(a)
    bh, bl = split2(b)
    return dot(ah, bh, dims) + (dot(ah, bl, dims) + dot(al, bh, dims))


def panel_kernel(momentum, gradient, right, out, mom_v, grad_v, right_v, sems):
    pieces = 2
    width = COLS // pieces
    copies = []
    for layer in range(LAYERS):
        for piece in range(pieces):
            cut = slice(piece * width, (piece + 1) * width)
            slot = len(copies)
            group = [
                pltpu.make_async_copy(momentum.at[layer, :, cut], mom_v.at[layer, :, cut], sems.at[slot, 0]),
                pltpu.make_async_copy(gradient.at[layer, :, cut], grad_v.at[layer, :, cut], sems.at[slot, 1]),
                pltpu.make_async_copy(right.at[layer, cut, :], right_v.at[layer, cut, :], sems.at[slot, 2]),
            ]
            for item in group:
                item.start()
            copies.append(group)
    for layer in range(LAYERS):
        total = jnp.zeros((ROWS, R), F32)
        for piece in range(pieces):
            for item in copies[layer * pieces + piece]:
                item.wait()
            cut = slice(piece * width, (piece + 1) * width)
            buffer = mom_v[layer, :, cut] + grad_v[layer, :, cut].astype(F32)
            factor = right_v[layer, cut, :]
            high, mid, low = split3(buffer)
            dims = ((1,), (0,))
            total += dot(high, factor, dims) + (dot(mid, factor, dims) + dot(low, factor, dims))
        out[layer] = total


def product(core, ids, panel_t, packed, layer, buffer, out):
    x = ids[1]
    for step in range(4):
        owner = core * 4 + lax.rem(x + step, 4)
        start = pl.multiple_of(owner * PIECE, PIECE)
        out[step, layer, 0:R] = dot_x3(panel_t, buffer[layer, :, pl.ds(start, PIECE)], ((1,), (0,)))
        out[step, layer, R:] = packed[layer, pl.ds(pl.multiple_of(owner * GRAM, GRAM), GRAM)]


def send_kernel(ids, p0, p1, p2, p3, buffer, panel, packed, out):
    for layer in range(LAYERS):
        whole = (p0[layer] + p1[layer]) + (p2[layer] + p3[layer])
        panel[layer] = whole
        gram = lax.dot_general(whole, whole, (((0,), (0,)), ((), ())), precision=HIGHEST, preferred_element_type=F32)
        packed[layer, :, 0:R] = gram[0 : R // 2]
        packed[layer, :, R:] = gram[R // 2 :]
        product(1 - ids[0], ids, whole.T, packed, layer, buffer, out)


def keep_kernel(ids, panel, packed, buffer, out):
    for layer in range(LAYERS):
        product(ids[0], ids, panel[layer].T, packed, layer, buffer, out)


def sum_x_kernel(ids, s0, r1, r2, r3, send, keep):
    low, high = ids[2], ids[3]
    for layer in range(LAYERS):
        for step in range(4):
            band = lax.rem(high + step, 4) * 2
            for out, bit in ((send, 1 - low), (keep, low)):
                rows = pl.ds(pl.multiple_of((band + bit) * BAND, BAND), BAND)
                total = (s0[layer, rows, :] + r1[layer, rows, :]) + (r2[layer, rows, :] + r3[layer, rows, :])
                out[layer, step * BAND : (step + 1) * BAND] = total
        gram = (s0[layer, R:] + r1[layer, R:]) + (r2[layer, R:] + r3[layer, R:])
        send[layer, 4 * BAND :] = gram
        keep[layer, 4 * BAND :] = gram


def solve_kernel(ids, a0, a1, a2, a3, b0, b1, b2, b3, inverse, reduced, squares, work):
    core, x = ids[0], ids[1]
    pieces = []
    for own, group in ((core, (a0, a1, a2, a3)), (1 - core, (b0, b1, b2, b3))):
        for step in range(4):
            pieces.append((own * 4 + lax.rem(x + 4 - step, 4), group[step]))
    for owner, piece in pieces:
        for half in range(2):
            start = pl.multiple_of(owner * GRAM + half * (R // 2), GRAM)
            for layer in range(LAYERS):
                work[layer, pl.ds(start, GRAM), 0:R] = piece[layer, R:, half * R : (half + 1) * R]
    factor(work, inverse)
    for layer in range(LAYERS):
        left = wide_left(inverse[layer])
        total = jnp.zeros((R, R), F32)
        for owner, piece in pieces:
            part = wide_dot(left, piece[layer, 0:R])
            reduced[layer, :, pl.ds(pl.multiple_of(owner * PIECE, PIECE), PIECE)] = part
            square = part * part
            total += square[:, 0:R] + square[:, R:]
        squares[layer] = jnp.broadcast_to(jnp.sum(total.T, axis=0, keepdims=True), (8, R))


def factor(work, out):
    rows_id = lax.broadcasted_iota(jnp.int32, (R, R), 0)
    cols_id = lax.broadcasted_iota(jnp.int32, (R, R), 1)
    unit = jnp.where(rows_id == cols_id, 1.0, 0.0).astype(F32)
    for layer in range(LAYERS):
        work[layer, :, R : 2 * R] = unit
    for base in range(0, R, BLOCK):
        for layer in range(LAYERS):
            rows = [work[layer, base + i : base + i + 1, :] for i in range(BLOCK)]
            square = [
                [jnp.broadcast_to(rows[i][:, base + j : base + j + 1], (1, 2 * R)) for j in range(i + 1)] for i in range(BLOCK)
            ]
            for j in range(BLOCK):
                pivot = square[j][j]
                inverse = lax.rsqrt(pivot)
                inverse = inverse * (1.5 - 0.5 * pivot * inverse * inverse)
                rows[j] = rows[j] * inverse
                for i in range(j + 1, BLOCK):
                    square[i][j] = square[i][j] * inverse
                for i in range(j + 1, BLOCK):
                    for k in range(j + 1, i + 1):
                        square[i][k] = square[i][k] - square[i][j] * square[k][j]
                    rows[i] = rows[i] - square[i][j] * rows[j]
            done = jnp.concatenate(rows, axis=0)
            out[layer, base : base + BLOCK, :] = done[:, R:]
            after = base + BLOCK
            if after < R:
                left = done[:, 0:R]
                lh, lm, ll = split3(left)
                dh, dm, dl = split3(done)
                stack_l = jnp.concatenate([lh, lm, lh, lm, ll, lh], axis=0)
                stack_d = jnp.concatenate([dh, dh, dm, dm, dh, dl], axis=0)
                change = dot(stack_l, stack_d, ((0,), (0,)))
                work[layer, after:, :] = work[layer, after:, :] - change[after:, :]


def spread_kernel(ids, gram, m0, m1, m2, m3, o0, o1, o2, o3, out):
    low, high = ids[2], ids[3]
    for bit, group in ((low, (m0, m1, m2, m3)), (1 - low, (o0, o1, o2, o3))):
        for step in range(4):
            band = lax.rem(high + 4 - step, 4) * 2 + bit
            rows = pl.ds(pl.multiple_of(band * BAND, BAND), BAND)
            for layer in range(LAYERS):
                out[layer, rows, :] = group[step][layer]
    out[:, R:] = gram[...]


def wide_left(a):
    high, low = split2(a)
    top = jnp.concatenate([high, high], axis=1)
    bottom = jnp.concatenate([low, jnp.zeros_like(low)], axis=1)
    return jnp.concatenate([top, bottom], axis=0)


def wide_dot(left, b):
    high, low = split2(b)
    both = dot(left, jnp.concatenate([high, low], axis=0), ((1,), (0,)))
    half = both.shape[0] // 2
    return both[0:half] + both[half:]


def momentum_kernel(panel, inverse, reduced, buffer, left, new_momentum, momentum_v, sems):
    width = 512
    copies = []
    for layer in range(LAYERS):
        basis = lax.dot_general(
            panel[layer], inverse[layer], (((1,), (1,)), ((), ())), precision=HIGHEST, preferred_element_type=F32
        )
        left[layer] = basis
        wide = wide_left(basis * 0.05)
        for start in range(0, COLS, width):
            cut = slice(start, start + width)
            change = wide_dot(wide, reduced[layer, :, cut])
            momentum_v[layer, :, cut] = buffer[layer, :, cut] - change
            copies.append(
                pltpu.make_async_copy(
                    momentum_v.at[layer, :, cut], new_momentum.at[layer, :, cut], sems.at[len(copies)]
                )
            )
            copies[-1].start()
    for item in copies:
        item.wait()


def weight_kernel(left, reduced, s0, s1, s2, s3, weight, new_weight, new_basis, weight_v, basis_v, in_sems, sems):
    width = 512
    loads = []
    copies = []
    for layer in range(LAYERS):
        for start in range(0, COLS, width):
            cut = slice(start, start + width)
            loads.append(
                pltpu.make_async_copy(weight.at[layer, :, cut], weight_v.at[layer, :, cut], in_sems.at[len(loads)])
            )
            loads[-1].start()
    for layer in range(LAYERS):
        squares = (s0[layer, 0:1, :] + s1[layer, 0:1, :]) + (s2[layer, 0:1, :] + s3[layer, 0:1, :])
        scale = lax.rsqrt(squares * (1.0 / D) + 1e-06)
        wide = wide_left(left[layer] * (scale * (0.05 * math.sqrt(D / R))))
        for start in range(0, COLS, width):
            cut = slice(start, start + width)
            part = reduced[layer, :, cut]
            change = wide_dot(wide, part)
            loads[len(copies)].wait()
            weight_v[layer, :, cut] = (1.0 - 0.05 * 0.1) * weight_v[layer, :, cut] - change
            basis_v[layer, cut, :] = (part.T * scale).astype(BF16)
            slot = len(copies)
            group = [
                pltpu.make_async_copy(weight_v.at[layer, :, cut], new_weight.at[layer, :, cut], sems.at[slot, 0]),
                pltpu.make_async_copy(basis_v.at[layer, cut, :], new_basis.at[layer, cut, :], sems.at[slot, 1]),
            ]
            for item in group:
                item.start()
            copies.append(group)
    for group in copies:
        for item in group:
            item.wait()


def place(z, x, core):
    return (z * 4 + x) * 2 + core


def fsdp_moves(dz, dx, flip_core=0, flip_z=0):
    return [
        (place(z, x, c), place(((z ^ flip_z) + dz) % 8, (x + dx) % 4, c ^ flip_core))
        for z in range(8)
        for x in range(4)
        for c in range(2)
    ]


def move_core(a):
    return lax.ppermute(a, "fsdp", fsdp_moves(0, 0, flip_core=1))


def move_x(a, step):
    return lax.ppermute(a, "fsdp", fsdp_moves(0, step))


def move_z(a, step):
    return lax.ppermute(a, "fsdp", fsdp_moves(step, 0))


def move_pair(a, flip_core=0):
    return lax.ppermute(a, "fsdp", fsdp_moves(0, 0, flip_core, 1))


def move_tp(a, step):
    return lax.ppermute(a, "tp", [(i, (i + step) % 4) for i in range(4)])


def body(weight, gradient, momentum, right_basis):
    index = lax.axis_index("fsdp")
    z = index // 8
    ids = jnp.stack([index % 2, (index // 2) % 4, z % 2, z // 2, lax.axis_index("tp")]).astype(jnp.int32)

    with jax.named_scope("panel"):
        part = call(
            panel_kernel, struct(LAYERS, ROWS, R), [HBM] * 3, (momentum, gradient, right_basis), 300 << 20, 4 << 20,
            scratch=[
                pltpu.VMEM((LAYERS, ROWS, COLS), F32), pltpu.VMEM((LAYERS, ROWS, COLS), BF16),
                pltpu.VMEM((LAYERS, COLS, R), BF16), pltpu.SemaphoreType.DMA((4, 3)),
            ],
            limit=107 << 19,
        )
        parts = [move_tp(part, step) for step in (1, 2, 3)]
        buffer = momentum + gradient.astype(F32)
    with jax.named_scope("product"):
        piece = struct(LAYERS, R + GRAM, PIECE)
        panel, packed, send = call(
            send_kernel, (struct(LAYERS, ROWS, R), struct(LAYERS, R // 2, PIECE), struct(4, *piece.shape)),
            [SM] + [VM] * 5, (ids, part, *parts, buffer), 300 << 20, 3 << 20,
        )
        keep = call(
            keep_kernel, struct(4, *piece.shape), [SM] + [VM] * 3, (ids, panel, packed, buffer), 300 << 20, 3 << 20
        )
        got = move_core(send)
        sums = [keep[step] + got[step] for step in range(4)]
    with jax.named_scope("scatter"):
        arrived = [move_x(sums[step], step) for step in (1, 2, 3)]
        z_send, z_keep = call(
            sum_x_kernel, (struct(LAYERS, 4 * BAND + GRAM, PIECE),) * 2, [SM] + [VM] * 4, (ids, sums[0], *arrived)
        )
        pair = z_keep + move_pair(z_send)
        gram = pair[:, 4 * BAND :]
        bands = [
            jnp.concatenate([pair[:, step * BAND : (step + 1) * BAND], gram], axis=1) for step in range(4)
        ]
        own = bands[0] + ((move_z(bands[1], 2) + move_z(bands[3], 6)) + move_z(bands[2], 4))
    with jax.named_scope("gather"):
        band, gram = own[:, 0:BAND], own[:, BAND:]
        mine = [band] + [move_z(band, 2 * step) for step in (1, 2, 3)]
        others = move_pair(jnp.stack(mine))
        whole = call(spread_kernel, piece, [SM] + [VM] * 9, (ids, gram, *mine, *[others[step] for step in range(4)]))
        group = [whole] + [move_x(whole, step) for step in (1, 2, 3)]
        across = [move_core(item) for item in group]
    with jax.named_scope("update"):
        inverse, reduced, squares = call(
            solve_kernel, (struct(LAYERS, R, R), struct(LAYERS, R, COLS), struct(LAYERS, 8, R)), [SM] + [VM] * 8,
            (ids, *group, *across), 600 << 20, scratch=[pltpu.VMEM((LAYERS, R, 2 * R), F32)],
        )
        shares = [squares] + [move_tp(squares, step) for step in (1, 2, 3)]
        left, new_momentum = call(
            momentum_kernel, (struct(LAYERS, ROWS, R), struct(LAYERS, ROWS, COLS)), [VM] * 4,
            (panel, inverse, reduced, buffer), 800 << 20, 4 << 20,
            scratch=[pltpu.VMEM((LAYERS, ROWS, COLS), F32), pltpu.SemaphoreType.DMA((8,))],
            out_specs=(VM, HBM),
        )
        new_weight, new_basis = call(
            weight_kernel, (struct(LAYERS, ROWS, COLS), struct(LAYERS, COLS, R, dtype=BF16)), [VM] * 6 + [HBM],
            (left, reduced, *shares, weight), 800 << 20, 6 << 20,
            scratch=[
                pltpu.VMEM((LAYERS, ROWS, COLS), F32), pltpu.VMEM((LAYERS, COLS, R), BF16),
                pltpu.SemaphoreType.DMA((8,)), pltpu.SemaphoreType.DMA((8, 2)),
            ],
            out_specs=(HBM,) * 2,
        )
    return (new_weight, new_momentum, new_basis)


def solution(mesh):
    return jax.shard_map(
        body,
        mesh=mesh,
        in_specs=(
            P(None, "fsdp", "tp"),
            P(None, "fsdp", "tp"),
            P(None, "fsdp", "tp"),
            P(None, "tp", None),
        ),
        out_specs=(P(None, "fsdp", "tp"), P(None, "fsdp", "tp"), P(None, "tp", None)),
        check_vma=False,
    )
```

```python
import math

import jax
import jax.numpy as jnp
from jax import lax
from jax.experimental import pallas as pl
from jax.experimental.pallas import tpu as pltpu
from jax.sharding import PartitionSpec as P

D = 8192
R = 128
LAYERS = 2
ROWS = 128
COLS = 2048
PIECE = 256
BAND = 16
GRAM = 32
CHUNK = 2 * BAND + 8
BLOCK = 8

HIGHEST = lax.Precision.HIGHEST
F32 = jnp.float32
BF16 = jnp.bfloat16

VM = pl.BlockSpec(memory_space=pltpu.VMEM)
SM = pl.BlockSpec(memory_space=pltpu.SMEM)
ANY = pl.BlockSpec(memory_space=pl.ANY)
HBM = pl.BlockSpec(memory_space=pltpu.HBM)


def struct(*shape, dtype=F32):
    return jax.ShapeDtypeStruct(shape, dtype)


def call(kernel, outs, ins, args, flops=1 << 20, nbytes=1 << 20, scratch=(), out_specs=None, limit=16 << 20):
    return pl.pallas_call(
        kernel,
        out_shape=outs,
        in_specs=ins,
        out_specs=out_specs or jax.tree.map(lambda _: VM, outs),
        scratch_shapes=list(scratch),
        compiler_params=pltpu.CompilerParams(vmem_limit_bytes=limit),
        cost_estimate=pl.CostEstimate(flops=flops, bytes_accessed=nbytes, transcendentals=0),
    )(*args)


def split2(a):
    high = a.astype(BF16)
    return high, (a - high.astype(F32)).astype(BF16)


def split3(a):
    high = a.astype(BF16)
    rest = a - high.astype(F32)
    mid = rest.astype(BF16)
    return high, mid, (rest - mid.astype(F32)).astype(BF16)


def dot(a, b, dims):
    return lax.dot_general(a, b, (dims, ((), ())), preferred_element_type=F32)


def dot_x3(a, b, dims):
    ah, al = split2(a)
    bh, bl = split2(b)
    return dot(ah, bh, dims) + (dot(ah, bl, dims) + dot(al, bh, dims))


def panel_kernel(momentum, gradient, right, out, mom_v, grad_v, right_v, sems):
    pieces = 2
    width = COLS // pieces
    copies = []
    for layer in range(LAYERS):
        for piece in range(pieces):
            cut = slice(piece * width, (piece + 1) * width)
            slot = len(copies)
            group = [
                pltpu.make_async_copy(momentum.at[layer, :, cut], mom_v.at[layer, :, cut], sems.at[slot, 0]),
                pltpu.make_async_copy(gradient.at[layer, :, cut], grad_v.at[layer, :, cut], sems.at[slot, 1]),
                pltpu.make_async_copy(right.at[layer, cut, :], right_v.at[layer, cut, :], sems.at[slot, 2]),
            ]
            for item in group:
                item.start()
            copies.append(group)
    for layer in range(LAYERS):
        total = jnp.zeros((ROWS, R), F32)
        for piece in range(pieces):
            for item in copies[layer * pieces + piece]:
                item.wait()
            cut = slice(piece * width, (piece + 1) * width)
            buffer = mom_v[layer, :, cut] + grad_v[layer, :, cut].astype(F32)
            factor = right_v[layer, cut, :]
            high, low = split2(buffer)
            total += dot(high, factor, ((1,), (0,))) + dot(low, factor, ((1,), (0,)))
        out[layer] = total


def chunk_of(ids, core, rel):
    return core * 4 + lax.bitwise_xor(ids[1], rel)


def columns(ids, core, rel):
    return pl.ds(pl.multiple_of(chunk_of(ids, core, rel) * PIECE, PIECE), PIECE)


FIRST, SECOND = (1, 3), (3, 1)
NEAR, FAR = [(0, rel) for rel in SECOND], [(rel, 2) for rel in FIRST]


def gram_of(panel):
    return lax.dot_general(panel, panel, (((0,), (0,)), ((), ())), precision=HIGHEST, preferred_element_type=F32)


def product(ids, core, rels, panel, buffer, outs):
    for layer, out in enumerate(outs):
        left = wide_left(panel[layer].T)
        for slot, rel in enumerate(rels[layer]):
            out[slot * R : (slot + 1) * R] = wide_dot(left, buffer[layer, :, columns(ids, core, rel)])


def begin_kernel(ids, p0, p1, p2, p3, buffer, panel, packed, out0, out1):
    for layer, out in enumerate((out0, out1)):
        whole = (p0[layer] + p1[layer]) + (p2[layer] + p3[layer])
        panel[layer] = whole
        gram = gram_of(whole)
        packed[layer, :, 0:R] = gram[0 : R // 2]
        packed[layer, :, R:] = gram[R // 2 :]
        out[2 * R :] = packed[layer, pl.ds(pl.multiple_of((1 - ids[0]) * GRAM, GRAM), GRAM)]
    product(ids, 1 - ids[0], FAR, panel, buffer, (out0, out1))


def begin_own_kernel(ids, panel, packed, buffer, out0, out1):
    for layer, out in enumerate((out0, out1)):
        out[2 * R :] = packed[layer, pl.ds(pl.multiple_of(ids[0] * GRAM, GRAM), GRAM)]
    product(ids, ids[0], FAR, panel, buffer, (out0, out1))


def rest_kernel(flip, ids, panel, buffer, out0, out1):
    product(ids, 1 - ids[0] if flip else ids[0], NEAR, panel, buffer, (out0, out1))


def sum_x_kernel(a0, b0, a1, b1, out):
    for layer, (left, right) in enumerate(((a0, b0), (a1, b1))):
        total = left[...] + right[...]
        for z in range(8):
            out[z, layer * BAND : (layer + 1) * BAND] = total[z * BAND : (z + 1) * BAND]
            start = 2 * BAND + 4 * layer
            out[z, start : start + 4] = total[R + 4 * z : R + 4 * z + 4]


def sum_z_kernel(got, out):
    total = (got[0] + got[1]) + (got[2] + got[3]) + ((got[4] + got[5]) + (got[6] + got[7]))
    for z in range(8):
        out[z] = total


def spread_kernel(got, out0, out1, gram):
    for layer, out in enumerate((out0, out1)):
        for z in range(8):
            out[z * BAND : (z + 1) * BAND] = got[z, layer * BAND : (layer + 1) * BAND]
            start = 2 * BAND + 4 * layer
            gram[layer, 4 * z : 4 * z + 4] = got[z, start : start + 4]


def factor_first_kernel(ids, own, other, out, work):
    core = ids[0]
    for index, gram in ((core, own), (1 - core, other)):
        for half in range(2):
            rows = pl.ds(pl.multiple_of(index * GRAM + half * (R // 2), GRAM), GRAM)
            for layer in range(LAYERS):
                work[layer, rows, :] = gram[layer, :, half * R : (half + 1) * R]
    factor(work, out, 0, R // 2)


def factor_second_kernel(first, before, out, work):
    for layer in range(LAYERS):
        work[layer, R // 2 :] = before[layer, R // 2 :]
        out[layer, 0 : R // 2] = first[layer, 0 : R // 2]
    factor(work, out, R // 2, R)


def factor(work, out, begin, end):
    lane = lax.broadcasted_iota(jnp.int32, (1, R), 1)
    for base in range(begin, end, BLOCK):
        after = base + BLOCK
        inside = (lane >= base) & (lane < after)
        for layer in range(LAYERS):
            rows = [work[layer, base + i : base + i + 1, :] for i in range(BLOCK)]
            square = [
                [jnp.broadcast_to(rows[i][:, base + j : base + j + 1], (1, R)) for j in range(i + 1)] for i in range(BLOCK)
            ]
            rows = [jnp.where(inside, jnp.where(lane == base + i, 1.0, 0.0), rows[i]) for i in range(BLOCK)]
            for j in range(BLOCK):
                pivot = square[j][j]
                inverse = lax.rsqrt(pivot)
                rows[j] = rows[j] * inverse
                for i in range(j + 1, BLOCK):
                    square[i][j] = square[i][j] * inverse
                for i in range(j + 1, BLOCK):
                    for k in range(j + 1, i + 1):
                        square[i][k] = square[i][k] - square[i][j] * square[k][j]
                    rows[i] = rows[i] - square[i][j] * rows[j]
            done = jnp.concatenate(rows, axis=0)
            out[layer, base:after, :] = jnp.where(lane < after, done, 0.0)
            if after < R:
                high, mid, low = split3(done)
                left = jnp.concatenate([high, mid, high, mid, low, high], axis=0)
                right = jnp.concatenate([high, high, mid, mid, high, low], axis=0)
                change = dot(left, right, ((0,), (0,)))
                work[layer, after:, :] = jnp.where(inside, 0.0, work[layer, after:, :]) - change[after:, :]


def wide_left(a):
    high, low = split2(a)
    top = jnp.concatenate([high, high], axis=1)
    bottom = jnp.concatenate([low, jnp.zeros_like(low)], axis=1)
    return jnp.concatenate([top, bottom], axis=0)


def wide_dot(left, b):
    high, low = split2(b)
    both = dot(left, jnp.concatenate([high, low], axis=0), ((1,), (0,)))
    half = both.shape[0] // 2
    return both[0:half] + both[half:]


def pieces(ids, layer, rels):
    return [
        (2 * side + slot, columns(ids, core, rel))
        for side, core in enumerate((ids[0], 1 - ids[0]))
        for slot, rel in enumerate(rels[layer])
    ]


def reduce_layer(left, own, other, reduced, layer):
    total = jnp.zeros((R, R), F32)
    for side, source in enumerate((own, other)):
        for slot in range(2):
            part = wide_dot(left, source[slot * R : (slot + 1) * R])
            reduced[layer, 2 * side + slot] = part
            square = part * part
            total += square[:, 0:R] + square[:, R:]
    return total


def update_momentum(ids, layer, rels, basis, reduced, buffer, new_momentum, staged, sems):
    wide = wide_left(basis * 0.05)
    copies = []
    for slot, cut in pieces(ids, layer, rels):
        staged[layer, slot] = buffer[layer, :, cut] - wide_dot(wide, reduced[layer, slot])
        copies.append(
            pltpu.make_async_copy(staged.at[layer, slot], new_momentum.at[layer, :, cut], sems.at[layer, slot])
        )
        copies[-1].start()
    return copies


def near_kernel(ids, panel, inverse, a0, a1, b0, b1, buffer, left, reduced, total, new_momentum, staged, sems):
    copies = []
    for layer, (own, other) in enumerate(((a0, b0), (a1, b1))):
        total[layer] = reduce_layer(wide_left(inverse[layer]), own, other, reduced, layer)
        basis = lax.dot_general(
            panel[layer], inverse[layer], (((1,), (1,)), ((), ())), precision=HIGHEST, preferred_element_type=F32
        )
        left[layer] = basis
        copies += update_momentum(ids, layer, NEAR, basis, reduced, buffer, new_momentum, staged, sems)
    for item in copies:
        item.wait()


def far_kernel(inverse, a0, a1, b0, b1, before, reduced, squares):
    for layer, (own, other) in enumerate(((a0, b0), (a1, b1))):
        total = before[layer] + reduce_layer(wide_left(inverse[layer]), own, other, reduced, layer)
        squares[layer] = jnp.broadcast_to(jnp.sum(total.T, axis=0, keepdims=True), (8, R))


def momentum_kernel(ids, left, reduced, buffer, begun, new_momentum, staged, sems):
    del begun
    copies = []
    for layer in range(LAYERS):
        copies += update_momentum(ids, layer, FAR, left[layer], reduced, buffer, new_momentum, staged, sems)
    for item in copies:
        item.wait()


def turn_kernel(ids, near, far, out):
    for layer in range(LAYERS):
        for rels, source in ((NEAR, near), (FAR, far)):
            for slot, cut in pieces(ids, layer, rels):
                out[layer, cut, :] = source[layer, slot].T


def weight_kernel(
    ids, left, near, far, turned, s0, s1, weight, new_weight, new_basis, weight_v, basis_v, sems, basis_sems
):
    copies = []
    for layer in range(LAYERS):
        squares = s0[layer, 0:1, :] + s1[layer, 0:1, :]
        scale = lax.rsqrt(squares * (1.0 / D) + 1e-06)
        wide = wide_left(left[layer] * (scale * (0.05 * math.sqrt(D / R))))
        for rels, source in ((NEAR, near), (FAR, far)):
            for slot, cut in pieces(ids, layer, rels):
                index = len(copies) - layer
                change = wide_dot(wide, source[layer, slot])
                weight_v[index] = (1.0 - 0.05 * 0.1) * weight[layer, :, cut] - change
                copies.append(pltpu.make_async_copy(weight_v.at[index], new_weight.at[layer, :, cut], sems.at[index]))
                copies[-1].start()
        basis_v[layer] = (turned[layer] * scale).astype(BF16)
        copies.append(pltpu.make_async_copy(basis_v.at[layer], new_basis.at[layer], basis_sems.at[layer]))
        copies[-1].start()
    for item in copies:
        item.wait()


def place(z, x, core):
    return (z * 4 + x) * 2 + core


def move_core(a):
    return lax.ppermute(a, "fsdp", [(i, i ^ 1) for i in range(64)])


def move_x(a, flip):
    moves = [(place(z, x, c), place(z, x ^ flip, c)) for z in range(8) for x in range(4) for c in range(2)]
    return lax.ppermute(a, "fsdp", moves)


def swap_z(a):
    groups = [[place(z, x, c) for z in range(8)] for x in range(4) for c in range(2)]
    return lax.all_to_all(a, "fsdp", 0, 0, axis_index_groups=groups, tiled=True)


def move_tp(a, flip):
    return lax.ppermute(a, "tp", [(i, i ^ flip) for i in range(4)])


def body(weight, gradient, momentum, right_basis):
    index = lax.axis_index("fsdp")
    core = index % 2
    ids = jnp.stack([core, (index // 2) % 4]).astype(jnp.int32)

    with jax.named_scope("panel"):
        part = call(
            panel_kernel, struct(LAYERS, ROWS, R), [HBM] * 3, (momentum, gradient, right_basis), 300 << 20, 4 << 20,
            scratch=[
                pltpu.VMEM((LAYERS, ROWS, COLS), F32), pltpu.VMEM((LAYERS, ROWS, COLS), BF16),
                pltpu.VMEM((LAYERS, COLS, R), BF16), pltpu.SemaphoreType.DMA((4, 3)),
            ],
            limit=107 << 19,
        )
        parts = [move_tp(part, flip) for flip in (3, 2, 1)]
        buffer = momentum + gradient.astype(F32)
    with jax.named_scope("product"):
        long, short = struct(2 * R + GRAM, PIECE), struct(2 * R, PIECE)
        panel, packed, *begun = call(
            begin_kernel, (struct(LAYERS, ROWS, R), struct(LAYERS, R // 2, PIECE), long, long), [SM] + [VM] * 5,
            (ids, part, *parts, buffer), 300 << 20, 3 << 20,
        )
        begun_own = call(
            begin_own_kernel, (long, long), [SM] + [VM] * 3, (ids, panel, packed, buffer), 300 << 20, 2 << 20
        )
        sends = [own + move_core(other) for own, other in zip(begun_own, begun)]
        rest, rest_own = [
            call(
                lambda *refs, flip=flip: rest_kernel(flip, *refs), (short, short), [SM] + [VM] * 2,
                (ids, panel, buffer), 300 << 20, 2 << 20,
            )
            for flip in (True, False)
        ]
    with jax.named_scope("scatter"):
        pairs = []
        for layer in range(LAYERS):
            send = sends[layer]
            got = move_x(send, FIRST[layer])
            gram = send[2 * R :] + got[2 * R :]
            keep = rest_own[layer] + move_core(rest[layer]) + got[0 : 2 * R]
            pairs += [
                jnp.concatenate([keep[0:R], gram]),
                move_x(jnp.concatenate([keep[R:], gram]), SECOND[layer]),
            ]
        chunks = swap_z(call(sum_x_kernel, struct(8, CHUNK, PIECE), [VM] * 4, pairs))
    with jax.named_scope("gather"):
        chunks = swap_z(call(sum_z_kernel, struct(8, CHUNK, PIECE), [VM], (chunks,)))
        *mine, gram = call(
            spread_kernel, (struct(R, PIECE), struct(R, PIECE), struct(LAYERS, GRAM, PIECE)), [VM], (chunks,)
        )
        inverse, work = call(
            factor_first_kernel, (struct(LAYERS, R, R), struct(LAYERS, R, R)), [SM] + [VM] * 2,
            (ids, gram, move_core(gram)), 3 << 30,
        )
        near = [jnp.concatenate([own, move_x(own, flip)]) for own, flip in zip(mine, SECOND)]
        inverse, *near = lax.optimization_barrier((inverse, *near))
        far = [move_x(pair, flip) for pair, flip in zip(near, FIRST)]
        near_other = [move_core(item) for item in near]
        inverse = call(
            factor_second_kernel, struct(LAYERS, R, R), [VM] * 2, (inverse, work), 3 << 30,
            scratch=[pltpu.VMEM((LAYERS, R, R), F32)],
        )
        four = struct(LAYERS, 4, R, PIECE)
        moved = struct(LAYERS, ROWS, COLS)
        staging = [pltpu.VMEM((LAYERS, 4, ROWS, PIECE), F32), pltpu.SemaphoreType.DMA((LAYERS, 4))]
        left, near_reduced, total, new_momentum = call(
            near_kernel, (struct(LAYERS, ROWS, R), four, struct(LAYERS, R, R), moved), [SM] + [VM] * 7,
            (ids, panel, inverse, *near, *near_other, buffer), 2 << 30, 3 << 20,
            scratch=staging, out_specs=(VM, VM, VM, HBM),
        )
        total, *far = lax.optimization_barrier((total, *far))
        far_other = [move_core(item) for item in far]
    with jax.named_scope("update"):
        far_reduced, squares = call(
            far_kernel, (four, struct(LAYERS, 8, R)), [VM] * 6, (inverse, *far, *far_other, total), 1 << 30,
        )
        got = move_tp(squares, 1)
        new_momentum = pl.pallas_call(
            momentum_kernel,
            out_shape=moved,
            in_specs=[SM] + [VM] * 3 + [HBM],
            out_specs=HBM,
            scratch_shapes=staging,
            input_output_aliases={4: 0},
            compiler_params=pltpu.CompilerParams(vmem_limit_bytes=16 << 20),
            cost_estimate=pl.CostEstimate(flops=1 << 30, bytes_accessed=2 << 20, transcendentals=0),
        )(ids, left, far_reduced, buffer, new_momentum)
        new_momentum, squares, got = lax.optimization_barrier((new_momentum, squares, got))
        squares = squares + got
        got = move_tp(squares, 3)
        turned = call(
            turn_kernel, struct(LAYERS, COLS, R), [SM] + [VM] * 2, (ids, near_reduced, far_reduced), 1 << 30, 4 << 20
        )
        turned, squares, got = lax.optimization_barrier((turned, squares, got))
        new_weight, new_basis = call(
            weight_kernel, (moved, struct(LAYERS, COLS, R, dtype=BF16)), [SM] + [VM] * 7,
            (ids, left, near_reduced, far_reduced, turned, squares, got, weight), 800 << 20, 6 << 20,
            scratch=[
                pltpu.VMEM((16, ROWS, PIECE), F32), pltpu.VMEM((LAYERS, COLS, R), BF16),
                pltpu.SemaphoreType.DMA((16,)), pltpu.SemaphoreType.DMA((LAYERS,)),
            ],
            out_specs=(HBM,) * 2,
        )
    return (new_weight, new_momentum, new_basis)


def solution(mesh):
    return jax.shard_map(
        body,
        mesh=mesh,
        in_specs=(
            P(None, "fsdp", "tp"),
            P(None, "fsdp", "tp"),
            P(None, "fsdp", "tp"),
            P(None, "tp", None),
        ),
        out_specs=(P(None, "fsdp", "tp"), P(None, "fsdp", "tp"), P(None, "tp", None)),
        check_vma=False,
    )
```

```python
import math

import jax
import jax.numpy as jnp
from jax import lax
from jax.experimental import pallas as pl
from jax.experimental.pallas import tpu as pltpu
from jax.sharding import PartitionSpec as P

D = 8192
R = 128
LAYERS = 2
ROWS = 128
COLS = 2048
PIECE = 256
BAND = 16
GRAM = 32
CHUNK = 2 * BAND + 8
BLOCK = 8

HIGHEST = lax.Precision.HIGHEST
F32 = jnp.float32
BF16 = jnp.bfloat16

VM = pl.BlockSpec(memory_space=pltpu.VMEM)
SM = pl.BlockSpec(memory_space=pltpu.SMEM)
ANY = pl.BlockSpec(memory_space=pl.ANY)
HBM = pl.BlockSpec(memory_space=pltpu.HBM)


def struct(*shape, dtype=F32):
    return jax.ShapeDtypeStruct(shape, dtype)


def call(kernel, outs, ins, args, flops=1 << 20, nbytes=1 << 20, scratch=(), out_specs=None, limit=16 << 20, aliases=None):
    return pl.pallas_call(
        kernel,
        out_shape=outs,
        in_specs=ins,
        out_specs=out_specs or jax.tree.map(lambda _: VM, outs),
        scratch_shapes=list(scratch),
        input_output_aliases=aliases or {},
        compiler_params=pltpu.CompilerParams(vmem_limit_bytes=limit),
        cost_estimate=pl.CostEstimate(flops=flops, bytes_accessed=nbytes, transcendentals=0),
    )(*args)


def split2(a):
    high = a.astype(BF16)
    return high, (a - high.astype(F32)).astype(BF16)


def split3(a):
    high = a.astype(BF16)
    rest = a - high.astype(F32)
    mid = rest.astype(BF16)
    return high, mid, (rest - mid.astype(F32)).astype(BF16)


def dot(a, b, dims):
    return lax.dot_general(a, b, (dims, ((), ())), preferred_element_type=F32)


def dot_x3(a, b, dims):
    ah, al = split2(a)
    bh, bl = split2(b)
    return dot(ah, bh, dims) + (dot(ah, bl, dims) + dot(al, bh, dims))


def panel_kernel(momentum, gradient, right, out, mom_v, grad_v, right_v, sems):
    pieces = 2
    width = COLS // pieces
    copies = []
    for layer in range(LAYERS):
        for piece in range(pieces):
            cut = slice(piece * width, (piece + 1) * width)
            slot = len(copies)
            group = [
                pltpu.make_async_copy(momentum.at[layer, :, cut], mom_v.at[layer, :, cut], sems.at[slot, 0]),
                pltpu.make_async_copy(gradient.at[layer, :, cut], grad_v.at[layer, :, cut], sems.at[slot, 1]),
                pltpu.make_async_copy(right.at[layer, cut, :], right_v.at[layer, cut, :], sems.at[slot, 2]),
            ]
            for item in group:
                item.start()
            copies.append(group)
    for layer in range(LAYERS):
        total = jnp.zeros((ROWS, R), F32)
        for piece in range(pieces):
            for item in copies[layer * pieces + piece]:
                item.wait()
            cut = slice(piece * width, (piece + 1) * width)
            buffer = mom_v[layer, :, cut] + grad_v[layer, :, cut].astype(F32)
            factor = right_v[layer, cut, :]
            both = dot(jnp.concatenate(split2(buffer), axis=0), factor, ((1,), (0,)))
            total += both[0:ROWS] + both[ROWS:]
        out[layer] = total


def chunk_of(ids, core, rel):
    return core * 4 + lax.bitwise_xor(ids[1], rel)


def columns(ids, core, rel):
    return pl.ds(pl.multiple_of(chunk_of(ids, core, rel) * PIECE, PIECE), PIECE)


FIRST, SECOND = (1, 3), (3, 1)
NEAR, FAR = [(0, rel) for rel in SECOND], [(rel, 2) for rel in FIRST]


def gram_of(panel):
    return lax.dot_general(panel, panel, (((0,), (0,)), ((), ())), precision=HIGHEST, preferred_element_type=F32)


def product(ids, core, rels, lefts, buffer, out):
    for layer in range(LAYERS):
        left = lefts[layer]
        for slot, rel in enumerate(rels[layer]):
            out[layer, slot * R : (slot + 1) * R] = wide_dot(left, buffer[layer, :, columns(ids, core, rel)])


def begin_kernel(ids, p0, p1, p2, p3, buffer, panel, lefts, packed, out):
    for layer in range(LAYERS):
        whole = (p0[layer] + p1[layer]) + (p2[layer] + p3[layer])
        panel[layer] = whole
        lefts[layer] = wide_left(whole.T)
        gram = gram_of(whole)
        packed[layer, :, 0:R] = gram[0 : R // 2]
        packed[layer, :, R:] = gram[R // 2 :]
        out[layer, 2 * R :] = packed[layer, pl.ds(pl.multiple_of((1 - ids[0]) * GRAM, GRAM), GRAM)]
    product(ids, 1 - ids[0], FAR, lefts, buffer, out)


def begin_own_kernel(ids, lefts, packed, buffer, out):
    for layer in range(LAYERS):
        out[layer, 2 * R :] = packed[layer, pl.ds(pl.multiple_of(ids[0] * GRAM, GRAM), GRAM)]
    product(ids, ids[0], FAR, lefts, buffer, out)


def rest_kernel(flip, ids, lefts, buffer, out):
    product(ids, 1 - ids[0] if flip else ids[0], NEAR, lefts, buffer, out)


def sum_x_kernel(a0, b0, a1, b1, out):
    for layer, (left, right) in enumerate(((a0, b0), (a1, b1))):
        total = left[...] + right[...]
        for z in range(8):
            out[z, layer * BAND : (layer + 1) * BAND] = total[z * BAND : (z + 1) * BAND]
            start = 2 * BAND + 4 * layer
            out[z, start : start + 4] = total[R + 4 * z : R + 4 * z + 4]


def sum_z_kernel(got, out):
    total = (got[0] + got[1]) + (got[2] + got[3]) + ((got[4] + got[5]) + (got[6] + got[7]))
    for z in range(8):
        out[z] = total


def spread_kernel(got, out, gram):
    for layer in range(LAYERS):
        for z in range(8):
            out[layer, z * BAND : (z + 1) * BAND] = got[z, layer * BAND : (layer + 1) * BAND]
            start = 2 * BAND + 4 * layer
            gram[layer, 4 * z : 4 * z + 4] = got[z, start : start + 4]


def factor_kernel(ids, own, other, out, work):
    core = ids[0]
    for index, gram in ((core, own), (1 - core, other)):
        for half in range(2):
            rows = pl.ds(pl.multiple_of(index * GRAM + half * (R // 2), GRAM), GRAM)
            for layer in range(LAYERS):
                work[layer, rows, :] = gram[layer, :, half * R : (half + 1) * R]
    factor(work, out, 0, R)


def factor(work, out, begin, end):
    lane = lax.broadcasted_iota(jnp.int32, (1, R), 1)
    for base in range(begin, end, BLOCK):
        after = base + BLOCK
        inside = (lane >= base) & (lane < after)
        rows = [
            jnp.concatenate([work[layer, base + i : base + i + 1, :] for layer in range(LAYERS)], axis=0)
            for i in range(BLOCK)
        ]
        square = [
            [jnp.broadcast_to(rows[i][:, base + j : base + j + 1], (LAYERS, R)) for j in range(i + 1)]
            for i in range(BLOCK)
        ]
        rows = [jnp.where(inside, jnp.where(lane == base + i, 1.0, 0.0), rows[i]) for i in range(BLOCK)]
        for j in range(BLOCK):
            inverse = lax.rsqrt(square[j][j])
            rows[j] = rows[j] * inverse
            for i in range(j + 1, BLOCK):
                square[i][j] = square[i][j] * inverse
            for i in range(j + 1, BLOCK):
                for k in range(j + 1, i + 1):
                    square[i][k] = square[i][k] - square[i][j] * square[k][j]
                rows[i] = rows[i] - square[i][j] * rows[j]
        for layer in range(LAYERS):
            done = jnp.concatenate([row[layer : layer + 1] for row in rows], axis=0)
            out[layer, base:after, :] = jnp.where(lane < after, done, 0.0)
            if after < R:
                high, mid, low = split3(done)
                left = jnp.concatenate([high, mid, high, mid, low, high], axis=0)
                right = jnp.concatenate([high, high, mid, mid, high, low], axis=0)
                change = dot(left, right, ((0,), (0,)))
                work[layer, after:, :] = jnp.where(inside, 0.0, work[layer, after:, :]) - change[after:, :]


def wide_left(a):
    high, low = split2(a)
    top = jnp.concatenate([high, high], axis=1)
    bottom = jnp.concatenate([low, jnp.zeros_like(low)], axis=1)
    return jnp.concatenate([top, bottom], axis=0)


def wide_dot(left, b):
    high, low = split2(b)
    both = dot(left, jnp.concatenate([high, low], axis=0), ((1,), (0,)))
    half = both.shape[0] // 2
    return both[0:half] + both[half:]


EARLY = [(0, 0), (0, 1), (0, 3)]
REST = [(0, 2), (1, 0), (1, 1), (1, 3), (1, 2)]


def spots(ids, where):
    return [(slot, columns(ids, 1 - ids[0] if side else ids[0], rel)) for slot, (side, rel) in enumerate(where)]


def reduce_layer(left, sources, reduced, layer):
    total = jnp.zeros((R, R), F32)
    for slot, source in enumerate(sources):
        part = wide_dot(left, source)
        reduced[layer, slot] = part
        square = part * part
        total += square[:, 0:R] + square[:, R:]
    return total


def update_momentum(ids, layer, where, basis, reduced, buffer, new_momentum, staged, sems):
    wide = wide_left(basis * 0.05)
    copies = []
    for slot, cut in spots(ids, where):
        staged[layer, slot] = buffer[layer, :, cut] - wide_dot(wide, reduced[layer, slot])
        copies.append(
            pltpu.make_async_copy(staged.at[layer, slot], new_momentum.at[layer, :, cut], sems.at[layer, slot])
        )
        copies[-1].start()
    return copies


def early_kernel(ids, panel, inverse, a0, a1, a3, buffer, left, reduced, total, new_momentum, staged, sems):
    copies = []
    for layer in range(LAYERS):
        sources = [piece[layer] for piece in (a0, a1, a3)]
        total[layer] = reduce_layer(wide_left(inverse[layer]), sources, reduced, layer)
        basis = lax.dot_general(
            panel[layer], inverse[layer], (((1,), (1,)), ((), ())), precision=HIGHEST, preferred_element_type=F32
        )
        left[layer] = basis
        copies += update_momentum(ids, layer, EARLY, basis, reduced, buffer, new_momentum, staged, sems)
    for item in copies:
        item.wait()


def rest_of_kernel(inverse, a20, a21, b0, b1, b3, b20, b21, before, reduced, squares):
    for layer, (own, other) in enumerate(((a20, b20), (a21, b21))):
        sources = [own[...], b0[layer], b1[layer], b3[layer], other[...]]
        total = before[layer] + reduce_layer(wide_left(inverse[layer]), sources, reduced, layer)
        squares[layer] = jnp.broadcast_to(jnp.sum(total.T, axis=0, keepdims=True), (8, R))


def momentum_kernel(ids, left, early, rest, buffer, begun, new_momentum, turned, staged, sems):
    del begun
    copies = []
    for layer in range(LAYERS):
        copies += update_momentum(ids, layer, REST, left[layer], rest, buffer, new_momentum, staged, sems)
    for layer in range(LAYERS):
        for where, source in ((EARLY, early), (REST, rest)):
            for slot, cut in spots(ids, where):
                turned[layer, cut, :] = source[layer, slot].T
    for item in copies:
        item.wait()


def weight_kernel(
    ids, left, early, rest, turned, s0, s1, s2, s3, weight, new_weight, new_basis, weight_v, basis_v, sems, basis_sems
):
    copies = []
    for layer in range(LAYERS):
        squares = (s0[layer, 0:1, :] + s1[layer, 0:1, :]) + (s2[layer, 0:1, :] + s3[layer, 0:1, :])
        scale = lax.rsqrt(squares * (1.0 / D) + 1e-06)
        wide = wide_left(left[layer] * (scale * (0.05 * math.sqrt(D / R))))
        for where, source in ((EARLY, early), (REST, rest)):
            for slot, cut in spots(ids, where):
                index = len(copies) - layer
                change = wide_dot(wide, source[layer, slot])
                weight_v[index] = (1.0 - 0.05 * 0.1) * weight[layer, :, cut] - change
                copies.append(pltpu.make_async_copy(weight_v.at[index], new_weight.at[layer, :, cut], sems.at[index]))
                copies[-1].start()
        basis_v[layer] = (turned[layer] * scale).astype(BF16)
        copies.append(pltpu.make_async_copy(basis_v.at[layer], new_basis.at[layer], basis_sems.at[layer]))
        copies[-1].start()
    for item in copies:
        item.wait()


def place(z, x, core):
    return (z * 4 + x) * 2 + core


def move_core(a):
    return lax.ppermute(a, "fsdp", [(i, i ^ 1) for i in range(64)])


def move_x(a, flip):
    moves = [(place(z, x, c), place(z, x ^ flip, c)) for z in range(8) for x in range(4) for c in range(2)]
    return lax.ppermute(a, "fsdp", moves)


def swap_z(a):
    groups = [[place(z, x, c) for z in range(8)] for x in range(4) for c in range(2)]
    return lax.all_to_all(a, "fsdp", 0, 0, axis_index_groups=groups, tiled=True)


def move_tp(a, flip):
    return lax.ppermute(a, "tp", [(i, i ^ flip) for i in range(4)])


def body(weight, gradient, momentum, right_basis):
    index = lax.axis_index("fsdp")
    core = index % 2
    ids = jnp.stack([core, (index // 2) % 4]).astype(jnp.int32)

    with jax.named_scope("panel"):
        part = call(
            panel_kernel, struct(LAYERS, ROWS, R), [HBM] * 3, (momentum, gradient, right_basis), 300 << 20, 4 << 20,
            scratch=[
                pltpu.VMEM((LAYERS, ROWS, COLS), F32), pltpu.VMEM((LAYERS, ROWS, COLS), BF16),
                pltpu.VMEM((LAYERS, COLS, R), BF16), pltpu.SemaphoreType.DMA((4, 3)),
            ],
            limit=107 << 19,
        )
        parts = [move_tp(part, flip) for flip in (3, 2, 1)]
        buffer = momentum + gradient.astype(F32)
    with jax.named_scope("product"):
        long, short = struct(LAYERS, 2 * R + GRAM, PIECE), struct(LAYERS, 2 * R, PIECE)
        panel, lefts, packed, begun = call(
            begin_kernel,
            (
                struct(LAYERS, ROWS, R), struct(LAYERS, 2 * R, 2 * R, dtype=BF16), struct(LAYERS, R // 2, PIECE),
                long,
            ),
            [SM] + [VM] * 5,
            (ids, part, *parts, buffer), 300 << 20, 3 << 20,
        )
        begun_own = call(
            begin_own_kernel, long, [SM] + [VM] * 3, (ids, lefts, packed, buffer), 300 << 20, 2 << 20
        )
        begun = move_core(begun)
        sends = [begun_own[layer] + begun[layer] for layer in range(LAYERS)]
        rest, rest_own = [
            call(
                lambda *refs, flip=flip: rest_kernel(flip, *refs), short, [SM] + [VM] * 2,
                (ids, lefts, buffer), 300 << 20, 2 << 20,
            )
            for flip in (True, False)
        ]
        rest = move_core(rest)
    with jax.named_scope("scatter"):
        pairs = []
        for layer in range(LAYERS):
            send = sends[layer]
            got = move_x(send, FIRST[layer])
            gram = send[2 * R :] + got[2 * R :]
            keep = rest_own[layer] + rest[layer] + got[0 : 2 * R]
            pairs += [
                jnp.concatenate([keep[0:R], gram]),
                move_x(jnp.concatenate([keep[R:], gram]), SECOND[layer]),
            ]
        chunks = swap_z(call(sum_x_kernel, struct(8, CHUNK, PIECE), [VM] * 4, pairs))
    with jax.named_scope("gather"):
        chunks = swap_z(call(sum_z_kernel, struct(8, CHUNK, PIECE), [VM], (chunks,)))
        whole, gram = call(spread_kernel, (struct(LAYERS, R, PIECE), struct(LAYERS, GRAM, PIECE)), [VM], (chunks,))
        group = [whole, move_x(whole, 1), move_x(whole, 3)]
        inverse = call(
            factor_kernel, struct(LAYERS, R, R), [SM] + [VM] * 2, (ids, gram, move_core(gram)), 8 << 30,
            scratch=[pltpu.VMEM((LAYERS, R, R), F32)],
        )
        inverse, *group[1:] = lax.optimization_barrier((inverse, *group[1:]))
        last = [move_x(group[2][0], 1), move_x(group[1][1], 3)]
        moved = struct(LAYERS, ROWS, COLS)

        def staging(count):
            return [pltpu.VMEM((LAYERS, count, ROWS, PIECE), F32), pltpu.SemaphoreType.DMA((LAYERS, count))]

        left, early, total, new_momentum = call(
            early_kernel,
            (struct(LAYERS, ROWS, R), struct(LAYERS, 3, R, PIECE), struct(LAYERS, R, R), moved), [SM] + [VM] * 6,
            (ids, panel, inverse, *group, buffer), 3 << 30, 3 << 20, scratch=staging(3), out_specs=(VM, VM, VM, HBM),
        )
        total, *last = lax.optimization_barrier((total, *last))
        total, *group[1:] = lax.optimization_barrier((total, *group[1:]))
        others = [move_core(item) for item in (*group, *last)]
    with jax.named_scope("update"):
        rest, squares = call(
            rest_of_kernel, (struct(LAYERS, 5, R, PIECE), struct(LAYERS, 8, R)), [VM] * 9,
            (inverse, *last, *others, total), 1 << 30,
        )
        shares = [squares] + [move_tp(squares, flip) for flip in (1, 2, 3)]
        new_momentum, turned = call(
            momentum_kernel, (moved, struct(LAYERS, COLS, R)), [SM] + [VM] * 4 + [HBM],
            (ids, left, early, rest, buffer, new_momentum), 3 << 30, 2 << 20,
            scratch=staging(5), out_specs=(HBM, VM), aliases={5: 0},
        )
        new_weight, new_basis = call(
            weight_kernel, (moved, struct(LAYERS, COLS, R, dtype=BF16)), [SM] + [VM] * 9,
            (ids, left, early, rest, turned, *shares, weight), 800 << 20, 6 << 20,
            scratch=[
                pltpu.VMEM((16, ROWS, PIECE), F32), pltpu.VMEM((LAYERS, COLS, R), BF16),
                pltpu.SemaphoreType.DMA((16,)), pltpu.SemaphoreType.DMA((LAYERS,)),
            ],
            out_specs=(HBM,) * 2,
        )
    return (new_weight, new_momentum, new_basis)


def solution(mesh):
    return jax.shard_map(
        body,
        mesh=mesh,
        in_specs=(
            P(None, "fsdp", "tp"),
            P(None, "fsdp", "tp"),
            P(None, "fsdp", "tp"),
            P(None, "tp", None),
        ),
        out_specs=(P(None, "fsdp", "tp"), P(None, "fsdp", "tp"), P(None, "tp", None)),
        check_vma=False,
    )
```

```python
import math

import jax
import jax.numpy as jnp
from jax import lax
from jax.experimental import pallas as pl
from jax.experimental.pallas import tpu as pltpu
from jax.sharding import PartitionSpec as P

D = 8192
R = 128
LAYERS = 2
ROWS = 128
COLS = 2048
PIECE = 256
BAND = 16
GRAM = 32
CHUNK = 2 * BAND + 8
BLOCK = 8

HIGHEST = lax.Precision.HIGHEST
F32 = jnp.float32
BF16 = jnp.bfloat16

VM = pl.BlockSpec(memory_space=pltpu.VMEM)
SM = pl.BlockSpec(memory_space=pltpu.SMEM)
ANY = pl.BlockSpec(memory_space=pl.ANY)
HBM = pl.BlockSpec(memory_space=pltpu.HBM)


def struct(*shape, dtype=F32):
    return jax.ShapeDtypeStruct(shape, dtype)


def call(kernel, outs, ins, args, flops=1 << 20, nbytes=1 << 20, scratch=(), out_specs=None, limit=16 << 20, aliases=None):
    return pl.pallas_call(
        kernel,
        out_shape=outs,
        in_specs=ins,
        out_specs=out_specs or jax.tree.map(lambda _: VM, outs),
        scratch_shapes=list(scratch),
        input_output_aliases=aliases or {},
        compiler_params=pltpu.CompilerParams(vmem_limit_bytes=limit),
        cost_estimate=pl.CostEstimate(flops=flops, bytes_accessed=nbytes, transcendentals=0),
    )(*args)


def split2(a):
    high = a.astype(BF16)
    return high, (a - high.astype(F32)).astype(BF16)


def split3(a):
    high = a.astype(BF16)
    rest = a - high.astype(F32)
    mid = rest.astype(BF16)
    return high, mid, (rest - mid.astype(F32)).astype(BF16)


def dot(a, b, dims):
    return lax.dot_general(a, b, (dims, ((), ())), preferred_element_type=F32)


def dot_x3(a, b, dims):
    ah, al = split2(a)
    bh, bl = split2(b)
    return dot(ah, bh, dims) + (dot(ah, bl, dims) + dot(al, bh, dims))


def panel_kernel(momentum, gradient, right, out, mom_v, grad_v, right_v, sems):
    pieces = 2
    width = COLS // pieces
    copies = []
    for layer in range(LAYERS):
        for piece in range(pieces):
            cut = slice(piece * width, (piece + 1) * width)
            slot = len(copies)
            group = [
                pltpu.make_async_copy(momentum.at[layer, :, cut], mom_v.at[layer, :, cut], sems.at[slot, 0]),
                pltpu.make_async_copy(gradient.at[layer, :, cut], grad_v.at[layer, :, cut], sems.at[slot, 1]),
                pltpu.make_async_copy(right.at[layer, cut, :], right_v.at[layer, cut, :], sems.at[slot, 2]),
            ]
            for item in group:
                item.start()
            copies.append(group)
    for layer in range(LAYERS):
        total = jnp.zeros((ROWS, R), F32)
        for piece in range(pieces):
            for item in copies[layer * pieces + piece]:
                item.wait()
            cut = slice(piece * width, (piece + 1) * width)
            buffer = mom_v[layer, :, cut] + grad_v[layer, :, cut].astype(F32)
            factor = right_v[layer, cut, :]
            both = dot(jnp.concatenate(split2(buffer), axis=0), factor, ((1,), (0,)))
            total += both[0:ROWS] + both[ROWS:]
        out[layer] = total


def chunk_of(ids, core, rel):
    return core * 4 + lax.bitwise_xor(ids[1], rel)


def columns(ids, core, rel):
    return pl.ds(pl.multiple_of(chunk_of(ids, core, rel) * PIECE, PIECE), PIECE)


FIRST = (1, 3)
FAR, REST_OF_X = (2,), (0, 1, 3)


def gram_of(panel):
    return lax.dot_general(panel, panel, (((0,), (0,)), ((), ())), precision=HIGHEST, preferred_element_type=F32)


def product(ids, core, rels, lefts, buffer, out):
    for layer in range(LAYERS):
        left = lefts[layer]
        for slot, rel in enumerate(rels):
            out[layer, slot * R : (slot + 1) * R] = wide_dot(left, buffer[layer, :, columns(ids, core, rel)])


def begin_kernel(ids, p0, p1, p2, p3, buffer, panel, lefts, packed, out):
    for layer in range(LAYERS):
        whole = (p0[layer] + p1[layer]) + (p2[layer] + p3[layer])
        panel[layer] = whole
        lefts[layer] = wide_left(whole.T)
        gram = gram_of(whole)
        packed[layer, :, 0:R] = gram[0 : R // 2]
        packed[layer, :, R:] = gram[R // 2 :]
        out[layer, R:] = packed[layer, pl.ds(pl.multiple_of((1 - ids[0]) * GRAM, GRAM), GRAM)]
    product(ids, 1 - ids[0], FAR, lefts, buffer, out)


def begin_own_kernel(ids, lefts, packed, buffer, out):
    for layer in range(LAYERS):
        out[layer, R:] = packed[layer, pl.ds(pl.multiple_of(ids[0] * GRAM, GRAM), GRAM)]
    product(ids, ids[0], FAR, lefts, buffer, out)


def rest_kernel(flip, ids, lefts, buffer, out):
    product(ids, 1 - ids[0] if flip else ids[0], REST_OF_X, lefts, buffer, out)


def sum_x_kernel(own, got1, got3, gram, out):
    for layer, last in enumerate((got3, got1)):
        rows = slice(layer * R, (layer + 1) * R)
        total = own[layer] + (got1[rows] + got3[rows])
        grams = gram[layer] + last[2 * R :]
        for z in range(8):
            out[z, layer * BAND : (layer + 1) * BAND] = total[z * BAND : (z + 1) * BAND]
            start = 2 * BAND + 4 * layer
            out[z, start : start + 4] = grams[4 * z : 4 * z + 4]


def sum_z_kernel(got, out):
    total = (got[0] + got[1]) + (got[2] + got[3]) + ((got[4] + got[5]) + (got[6] + got[7]))
    for z in range(8):
        out[z] = total


def spread_kernel(got, out, gram):
    for layer in range(LAYERS):
        for z in range(8):
            out[layer, z * BAND : (z + 1) * BAND] = got[z, layer * BAND : (layer + 1) * BAND]
            start = 2 * BAND + 4 * layer
            gram[layer, 4 * z : 4 * z + 4] = got[z, start : start + 4]


def factor_kernel(ids, own, other, out, work):
    core = ids[0]
    for index, gram in ((core, own), (1 - core, other)):
        for half in range(2):
            rows = pl.ds(pl.multiple_of(index * GRAM + half * (R // 2), GRAM), GRAM)
            for layer in range(LAYERS):
                work[layer, rows, :] = gram[layer, :, half * R : (half + 1) * R]
    factor(work, out, 0, R)


def factor(work, out, begin, end):
    lane = lax.broadcasted_iota(jnp.int32, (1, R), 1)
    for base in range(begin, end, BLOCK):
        after = base + BLOCK
        inside = (lane >= base) & (lane < after)
        rows = [
            jnp.concatenate([work[layer, base + i : base + i + 1, :] for layer in range(LAYERS)], axis=0)
            for i in range(BLOCK)
        ]
        square = [
            [jnp.broadcast_to(rows[i][:, base + j : base + j + 1], (LAYERS, R)) for j in range(i + 1)]
            for i in range(BLOCK)
        ]
        rows = [jnp.where(inside, jnp.where(lane == base + i, 1.0, 0.0), rows[i]) for i in range(BLOCK)]
        for j in range(BLOCK):
            inverse = lax.rsqrt(square[j][j])
            rows[j] = rows[j] * inverse
            for i in range(j + 1, BLOCK):
                square[i][j] = square[i][j] * inverse
            for i in range(j + 1, BLOCK):
                for k in range(j + 1, i + 1):
                    square[i][k] = square[i][k] - square[i][j] * square[k][j]
                rows[i] = rows[i] - square[i][j] * rows[j]
        for layer in range(LAYERS):
            done = jnp.concatenate([row[layer : layer + 1] for row in rows], axis=0)
            out[layer, base:after, :] = jnp.where(lane < after, done, 0.0)
            if after < R:
                high, mid, low = split3(done)
                left = jnp.concatenate([high, mid, high, mid, low, high], axis=0)
                right = jnp.concatenate([high, high, mid, mid, high, low], axis=0)
                change = dot(left, right, ((0,), (0,)))
                work[layer, after:, :] = jnp.where(inside, 0.0, work[layer, after:, :]) - change[after:, :]


def wide_left(a):
    high, low = split2(a)
    top = jnp.concatenate([high, high], axis=1)
    bottom = jnp.concatenate([low, jnp.zeros_like(low)], axis=1)
    return jnp.concatenate([top, bottom], axis=0)


def wide_dot(left, b):
    high, low = split2(b)
    both = dot(left, jnp.concatenate([high, low], axis=0), ((1,), (0,)))
    half = both.shape[0] // 2
    return both[0:half] + both[half:]


EARLY = [(0, 0), (0, 1), (0, 3)]
REST = [(0, 2), (1, 0), (1, 1), (1, 3), (1, 2)]


def spots(ids, where):
    return [(slot, columns(ids, 1 - ids[0] if side else ids[0], rel)) for slot, (side, rel) in enumerate(where)]


def reduce_layer(left, sources, reduced, layer):
    total = jnp.zeros((R, R), F32)
    for slot, source in enumerate(sources):
        part = wide_dot(left, source)
        reduced[layer, slot] = part
        square = part * part
        total += square[:, 0:R] + square[:, R:]
    return total


def update_momentum(ids, layer, where, basis, reduced, buffer, new_momentum, staged, sems):
    wide = wide_left(basis * 0.05)
    copies = []
    for slot, cut in spots(ids, where):
        staged[layer, slot] = buffer[layer, :, cut] - wide_dot(wide, reduced[layer, slot])
        copies.append(
            pltpu.make_async_copy(staged.at[layer, slot], new_momentum.at[layer, :, cut], sems.at[layer, slot])
        )
        copies[-1].start()
    return copies


def early_kernel(ids, panel, inverse, a0, a1, a3, buffer, left, reduced, total, new_momentum, staged, sems):
    copies = []
    for layer in range(LAYERS):
        sources = [piece[layer] for piece in (a0, a1, a3)]
        total[layer] = reduce_layer(wide_left(inverse[layer]), sources, reduced, layer)
        basis = lax.dot_general(
            panel[layer], inverse[layer], (((1,), (1,)), ((), ())), precision=HIGHEST, preferred_element_type=F32
        )
        left[layer] = basis
        copies += update_momentum(ids, layer, EARLY, basis, reduced, buffer, new_momentum, staged, sems)
    for item in copies:
        item.wait()


def rest_of_kernel(inverse, a20, a21, b0, b1, b3, b20, b21, before, reduced, squares):
    for layer, (own, other) in enumerate(((a20, b20), (a21, b21))):
        sources = [own[...], b0[layer], b1[layer], b3[layer], other[...]]
        total = before[layer] + reduce_layer(wide_left(inverse[layer]), sources, reduced, layer)
        squares[layer] = jnp.broadcast_to(jnp.sum(total.T, axis=0, keepdims=True), (8, R))


def momentum_kernel(ids, left, early, rest, buffer, begun, new_momentum, turned, staged, sems):
    del begun
    copies = []
    for layer in range(LAYERS):
        copies += update_momentum(ids, layer, REST, left[layer], rest, buffer, new_momentum, staged, sems)
    for layer in range(LAYERS):
        for where, source in ((EARLY, early), (REST, rest)):
            for slot, cut in spots(ids, where):
                turned[layer, cut, :] = source[layer, slot].T
    for item in copies:
        item.wait()


def weight_kernel(
    ids, left, early, rest, turned, s0, s1, s2, s3, weight, new_weight, new_basis, weight_v, basis_v, sems, basis_sems
):
    copies = []
    for layer in range(LAYERS):
        squares = (s0[layer, 0:1, :] + s1[layer, 0:1, :]) + (s2[layer, 0:1, :] + s3[layer, 0:1, :])
        scale = lax.rsqrt(squares * (1.0 / D) + 1e-06)
        wide = wide_left(left[layer] * (scale * (0.05 * math.sqrt(D / R))))
        for where, source in ((EARLY, early), (REST, rest)):
            for slot, cut in spots(ids, where):
                index = len(copies) - layer
                change = wide_dot(wide, source[layer, slot])
                weight_v[index] = (1.0 - 0.05 * 0.1) * weight[layer, :, cut] - change
                copies.append(pltpu.make_async_copy(weight_v.at[index], new_weight.at[layer, :, cut], sems.at[index]))
                copies[-1].start()
        basis_v[layer] = (turned[layer] * scale).astype(BF16)
        copies.append(pltpu.make_async_copy(basis_v.at[layer], new_basis.at[layer], basis_sems.at[layer]))
        copies[-1].start()
    for item in copies:
        item.wait()


def place(z, x, core):
    return (z * 4 + x) * 2 + core


def move_core(a):
    return lax.ppermute(a, "fsdp", [(i, i ^ 1) for i in range(64)])


def move_x(a, flip):
    moves = [(place(z, x, c), place(z, x ^ flip, c)) for z in range(8) for x in range(4) for c in range(2)]
    return lax.ppermute(a, "fsdp", moves)


def swap_z(a):
    groups = [[place(z, x, c) for z in range(8)] for x in range(4) for c in range(2)]
    return lax.all_to_all(a, "fsdp", 0, 0, axis_index_groups=groups, tiled=True)


def move_tp(a, flip):
    return lax.ppermute(a, "tp", [(i, i ^ flip) for i in range(4)])


def body(weight, gradient, momentum, right_basis):
    index = lax.axis_index("fsdp")
    core = index % 2
    ids = jnp.stack([core, (index // 2) % 4]).astype(jnp.int32)

    with jax.named_scope("panel"):
        part = call(
            panel_kernel, struct(LAYERS, ROWS, R), [HBM] * 3, (momentum, gradient, right_basis), 300 << 20, 4 << 20,
            scratch=[
                pltpu.VMEM((LAYERS, ROWS, COLS), F32), pltpu.VMEM((LAYERS, ROWS, COLS), BF16),
                pltpu.VMEM((LAYERS, COLS, R), BF16), pltpu.SemaphoreType.DMA((4, 3)),
            ],
            limit=107 << 19,
        )
        parts = [move_tp(part, flip) for flip in (1, 3, 2)]
        buffer = momentum + gradient.astype(F32)
    with jax.named_scope("product"):
        long, short = struct(LAYERS, R + GRAM, PIECE), struct(LAYERS, 3 * R, PIECE)
        panel, lefts, packed, begun = call(
            begin_kernel,
            (
                struct(LAYERS, ROWS, R), struct(LAYERS, 2 * R, 2 * R, dtype=BF16), struct(LAYERS, R // 2, PIECE),
                long,
            ),
            [SM] + [VM] * 5,
            (ids, part, *parts, buffer), 300 << 20, 3 << 20,
        )
        begun_own = call(
            begin_own_kernel, long, [SM] + [VM] * 3, (ids, lefts, packed, buffer), 300 << 20, 2 << 20
        )
        begun = move_core(begun)
        sends = [begun_own[layer] + begun[layer] for layer in range(LAYERS)]
        rest, rest_own = [
            call(
                lambda *refs, flip=flip: rest_kernel(flip, *refs), short, [SM] + [VM] * 2,
                (ids, lefts, buffer), 300 << 20, 2 << 20,
            )
            for flip in (True, False)
        ]
        rest = move_core(rest)
    with jax.named_scope("scatter"):
        got = [move_x(send, flip) for send, flip in zip(sends, FIRST)]
        gram = jnp.stack([send[R:] + more[R:] for send, more in zip(sends, got)])
        rest = rest_own + rest
        own, to1, to3 = rest[:, 0:R], rest[:, R : 2 * R], rest[:, 2 * R :]
        to1 = jnp.concatenate([to1[0], to1[1] + got[1][0:R], gram[1]])
        to3 = jnp.concatenate([to3[0] + got[0][0:R], to3[1], gram[0]])
        chunks = call(sum_x_kernel, struct(8, CHUNK, PIECE), [VM] * 4, (own, move_x(to1, 1), move_x(to3, 3), gram))
        chunks = swap_z(chunks)
    with jax.named_scope("gather"):
        chunks = swap_z(call(sum_z_kernel, struct(8, CHUNK, PIECE), [VM], (chunks,)))
        whole, gram = call(spread_kernel, (struct(LAYERS, R, PIECE), struct(LAYERS, GRAM, PIECE)), [VM], (chunks,))
        group = [whole, move_x(whole, 1), move_x(whole, 3)]
        inverse = call(
            factor_kernel, struct(LAYERS, R, R), [SM] + [VM] * 2, (ids, gram, move_core(gram)), 8 << 30,
            scratch=[pltpu.VMEM((LAYERS, R, R), F32)],
        )
        inverse, *group[1:] = lax.optimization_barrier((inverse, *group[1:]))
        last = [move_x(group[2][0], 1), move_x(group[1][1], 3)]
        moved = struct(LAYERS, ROWS, COLS)

        def staging(count):
            return [pltpu.VMEM((LAYERS, count, ROWS, PIECE), F32), pltpu.SemaphoreType.DMA((LAYERS, count))]

        left, early, total, new_momentum = call(
            early_kernel,
            (struct(LAYERS, ROWS, R), struct(LAYERS, 3, R, PIECE), struct(LAYERS, R, R), moved), [SM] + [VM] * 6,
            (ids, panel, inverse, *group, buffer), 3 << 30, 3 << 20, scratch=staging(3), out_specs=(VM, VM, VM, HBM),
        )
        total, *last = lax.optimization_barrier((total, *last))
        total, *group[1:] = lax.optimization_barrier((total, *group[1:]))
        others = [move_core(item) for item in (*group, *last)]
    with jax.named_scope("update"):
        rest, squares = call(
            rest_of_kernel, (struct(LAYERS, 5, R, PIECE), struct(LAYERS, 8, R)), [VM] * 9,
            (inverse, *last, *others, total), 1 << 30,
        )
        shares = [squares] + [move_tp(squares, flip) for flip in (1, 2, 3)]
        new_momentum, turned = call(
            momentum_kernel, (moved, struct(LAYERS, COLS, R)), [SM] + [VM] * 4 + [HBM],
            (ids, left, early, rest, buffer, new_momentum), 3 << 30, 2 << 20,
            scratch=staging(5), out_specs=(HBM, VM), aliases={5: 0},
        )
        new_weight, new_basis = call(
            weight_kernel, (moved, struct(LAYERS, COLS, R, dtype=BF16)), [SM] + [VM] * 9,
            (ids, left, early, rest, turned, *shares, weight), 800 << 20, 6 << 20,
            scratch=[
                pltpu.VMEM((16, ROWS, PIECE), F32), pltpu.VMEM((LAYERS, COLS, R), BF16),
                pltpu.SemaphoreType.DMA((16,)), pltpu.SemaphoreType.DMA((LAYERS,)),
            ],
            out_specs=(HBM,) * 2,
        )
    return (new_weight, new_momentum, new_basis)


def solution(mesh):
    return jax.shard_map(
        body,
        mesh=mesh,
        in_specs=(
            P(None, "fsdp", "tp"),
            P(None, "fsdp", "tp"),
            P(None, "fsdp", "tp"),
            P(None, "tp", None),
        ),
        out_specs=(P(None, "fsdp", "tp"), P(None, "fsdp", "tp"), P(None, "tp", None)),
        check_vma=False,
    )
```

```python
import math

import jax
import jax.numpy as jnp
from jax import lax
from jax.experimental import pallas as pl
from jax.experimental.pallas import tpu as pltpu
from jax.sharding import PartitionSpec as P

D = 8192
R = 128
LAYERS = 2
ROWS = 128
COLS = 2048
PIECE = 256
BAND = 16
GRAM = 32
CHUNK = 2 * BAND + 8
BLOCK = 8

HIGHEST = lax.Precision.HIGHEST
F32 = jnp.float32
BF16 = jnp.bfloat16

VM = pl.BlockSpec(memory_space=pltpu.VMEM)
SM = pl.BlockSpec(memory_space=pltpu.SMEM)
ANY = pl.BlockSpec(memory_space=pl.ANY)
HBM = pl.BlockSpec(memory_space=pltpu.HBM)


def struct(*shape, dtype=F32):
    return jax.ShapeDtypeStruct(shape, dtype)


def call(kernel, outs, ins, args, flops=1 << 20, nbytes=1 << 20, scratch=(), out_specs=None, limit=16 << 20, aliases=None):
    return pl.pallas_call(
        kernel,
        out_shape=outs,
        in_specs=ins,
        out_specs=out_specs or jax.tree.map(lambda _: VM, outs),
        scratch_shapes=list(scratch),
        input_output_aliases=aliases or {},
        compiler_params=pltpu.CompilerParams(vmem_limit_bytes=limit),
        cost_estimate=pl.CostEstimate(flops=flops, bytes_accessed=nbytes, transcendentals=0),
    )(*args)


def split2(a):
    high = a.astype(BF16)
    return high, (a - high.astype(F32)).astype(BF16)


def split3(a):
    high = a.astype(BF16)
    rest = a - high.astype(F32)
    mid = rest.astype(BF16)
    return high, mid, (rest - mid.astype(F32)).astype(BF16)


def dot(a, b, dims):
    return lax.dot_general(a, b, (dims, ((), ())), preferred_element_type=F32)


def dot_x3(a, b, dims):
    ah, al = split2(a)
    bh, bl = split2(b)
    return dot(ah, bh, dims) + (dot(ah, bl, dims) + dot(al, bh, dims))


def panel_kernel(momentum, gradient, right, out, mom_v, grad_v, right_v, sems):
    pieces = 2
    width = COLS // pieces
    copies = []
    for layer in range(LAYERS):
        for piece in range(pieces):
            cut = slice(piece * width, (piece + 1) * width)
            slot = len(copies)
            group = [
                pltpu.make_async_copy(momentum.at[layer, :, cut], mom_v.at[layer, :, cut], sems.at[slot, 0]),
                pltpu.make_async_copy(gradient.at[layer, :, cut], grad_v.at[layer, :, cut], sems.at[slot, 1]),
                pltpu.make_async_copy(right.at[layer, cut, :], right_v.at[layer, cut, :], sems.at[slot, 2]),
            ]
            for item in group:
                item.start()
            copies.append(group)
    for layer in range(LAYERS):
        total = jnp.zeros((ROWS, R), F32)
        for piece in range(pieces):
            for item in copies[layer * pieces + piece]:
                item.wait()
            cut = slice(piece * width, (piece + 1) * width)
            buffer = mom_v[layer, :, cut] + grad_v[layer, :, cut].astype(F32)
            factor = right_v[layer, cut, :]
            both = dot(jnp.concatenate(split2(buffer), axis=0), factor, ((1,), (0,)))
            total += both[0:ROWS] + both[ROWS:]
        out[layer] = total


def chunk_of(ids, core, rel):
    return core * 4 + lax.bitwise_xor(ids[1], rel)


def columns(ids, core, rel):
    return pl.ds(pl.multiple_of(chunk_of(ids, core, rel) * PIECE, PIECE), PIECE)


FIRST = (1, 3)
FAR, REST_OF_X = (2,), (0, 1, 3)


def gram_of(panel):
    return lax.dot_general(panel, panel, (((0,), (0,)), ((), ())), precision=HIGHEST, preferred_element_type=F32)


def product(ids, core, rels, lefts, buffer, out):
    for layer in range(LAYERS):
        left = lefts[layer]
        for slot, rel in enumerate(rels):
            out[layer, slot * R : (slot + 1) * R] = wide_dot(left, buffer[layer, :, columns(ids, core, rel)])


def begin_kernel(ids, p0, p1, p2, p3, buffer, panel, lefts, packed, out):
    for layer in range(LAYERS):
        whole = (p0[layer] + p1[layer]) + (p2[layer] + p3[layer])
        panel[layer] = whole
        lefts[layer] = wide_left(whole.T)
        gram = gram_of(whole)
        packed[layer, :, 0:R] = gram[0 : R // 2]
        packed[layer, :, R:] = gram[R // 2 :]
        out[layer, R:] = packed[layer, pl.ds(pl.multiple_of((1 - ids[0]) * GRAM, GRAM), GRAM)]
    product(ids, 1 - ids[0], FAR, lefts, buffer, out)


def begin_own_kernel(ids, lefts, packed, buffer, out):
    for layer in range(LAYERS):
        out[layer, R:] = packed[layer, pl.ds(pl.multiple_of(ids[0] * GRAM, GRAM), GRAM)]
    product(ids, ids[0], FAR, lefts, buffer, out)


def rest_kernel(flip, ids, lefts, buffer, out):
    product(ids, 1 - ids[0] if flip else ids[0], REST_OF_X, lefts, buffer, out)


def sum_x_kernel(own, got1, got3, gram, out):
    for layer, last in enumerate((got3, got1)):
        rows = slice(layer * R, (layer + 1) * R)
        total = own[layer] + (got1[rows] + got3[rows])
        grams = gram[layer] + last[2 * R :]
        for z in range(8):
            out[z, layer * BAND : (layer + 1) * BAND] = total[z * BAND : (z + 1) * BAND]
            start = 2 * BAND + 4 * layer
            out[z, start : start + 4] = grams[4 * z : 4 * z + 4]


def sum_z_kernel(got, out):
    total = (got[0] + got[1]) + (got[2] + got[3]) + ((got[4] + got[5]) + (got[6] + got[7]))
    for z in range(8):
        out[z] = total


def spread_kernel(got, out, gram):
    for layer in range(LAYERS):
        for z in range(8):
            out[layer, z * BAND : (z + 1) * BAND] = got[z, layer * BAND : (layer + 1) * BAND]
            start = 2 * BAND + 4 * layer
            gram[layer, 4 * z : 4 * z + 4] = got[z, start : start + 4]


def factor_kernel(ids, own, other, out, work):
    core = ids[0]
    for index, gram in ((core, own), (1 - core, other)):
        for half in range(2):
            rows = pl.ds(pl.multiple_of(index * GRAM + half * (R // 2), GRAM), GRAM)
            for layer in range(LAYERS):
                work[layer, rows, :] = gram[layer, :, half * R : (half + 1) * R]
    factor(work, out, 0, R)


def factor(work, out, begin, end):
    lane = lax.broadcasted_iota(jnp.int32, (1, R), 1)
    for base in range(begin, end, BLOCK):
        after = base + BLOCK
        inside = (lane >= base) & (lane < after)
        rows = [
            jnp.concatenate([work[layer, base + i : base + i + 1, :] for layer in range(LAYERS)], axis=0)
            for i in range(BLOCK)
        ]
        square = [
            [jnp.broadcast_to(rows[i][:, base + j : base + j + 1], (LAYERS, R)) for j in range(i + 1)]
            for i in range(BLOCK)
        ]
        rows = [jnp.where(inside, jnp.where(lane == base + i, 1.0, 0.0), rows[i]) for i in range(BLOCK)]
        for j in range(BLOCK):
            inverse = lax.rsqrt(square[j][j])
            rows[j] = rows[j] * inverse
            for i in range(j + 1, BLOCK):
                square[i][j] = square[i][j] * inverse
            for i in range(j + 1, BLOCK):
                for k in range(j + 1, i + 1):
                    square[i][k] = square[i][k] - square[i][j] * square[k][j]
                rows[i] = rows[i] - square[i][j] * rows[j]
        for layer in range(LAYERS):
            done = jnp.concatenate([row[layer : layer + 1] for row in rows], axis=0)
            out[layer, base:after, :] = jnp.where(lane < after, done, 0.0)
            if after < R:
                high, mid, low = split3(done)
                left = jnp.concatenate([high, mid, high, mid, low, high], axis=0)
                right = jnp.concatenate([high, high, mid, mid, high, low], axis=0)
                change = dot(left, right, ((0,), (0,)))
                work[layer, after:, :] = jnp.where(inside, 0.0, work[layer, after:, :]) - change[after:, :]


def wide_left(a):
    high, low = split2(a)
    top = jnp.concatenate([high, high], axis=1)
    bottom = jnp.concatenate([low, jnp.zeros_like(low)], axis=1)
    return jnp.concatenate([top, bottom], axis=0)


def stacked(b):
    return jnp.concatenate(split2(b), axis=0)


def stacked_dot(left, b):
    both = dot(left, b, ((1,), (0,)))
    half = both.shape[0] // 2
    return both[0:half] + both[half:]


def wide_dot(left, b):
    return stacked_dot(left, stacked(b))


EARLY = [(0, 0), (0, 1), (0, 3), (1, 0)]
REST = [(0, 2), (1, 1), (1, 3), (1, 2)]


def spots(ids, where):
    return [(slot, columns(ids, 1 - ids[0] if side else ids[0], rel)) for slot, (side, rel) in enumerate(where)]


def reduce_layer(left, sources, reduced, layer):
    total = jnp.zeros((R, R), F32)
    for slot, source in enumerate(sources):
        part = wide_dot(left, source)
        reduced[layer, slot] = stacked(part)
        square = part * part
        total += square[:, 0:R] + square[:, R:]
    return total


def update_momentum(ids, layer, where, basis, reduced, buffer, new_momentum, staged, sems):
    wide = wide_left(basis * 0.05)
    copies = []
    for slot, cut in spots(ids, where):
        staged[layer, slot] = buffer[layer, :, cut] - stacked_dot(wide, reduced[layer, slot])
        copies.append(
            pltpu.make_async_copy(staged.at[layer, slot], new_momentum.at[layer, :, cut], sems.at[layer, slot])
        )
        copies[-1].start()
    return copies


def turn(reduced, turned):
    for layer in range(LAYERS):
        for slot in range(4):
            turned[layer, slot] = (reduced[layer, slot, 0:R].astype(F32) + reduced[layer, slot, R:].astype(F32)).T


def early_kernel(
    ids, panel, inverse, a0, a1, a3, b0, buffer, left, reduced, total, turned, new_momentum, staged, sems
):
    copies = []
    for layer in range(LAYERS):
        sources = [piece[layer] for piece in (a0, a1, a3, b0)]
        total[layer] = reduce_layer(wide_left(inverse[layer]), sources, reduced, layer)
        basis = lax.dot_general(
            panel[layer], inverse[layer], (((1,), (1,)), ((), ())), precision=HIGHEST, preferred_element_type=F32
        )
        left[layer] = basis
        copies += update_momentum(ids, layer, EARLY, basis, reduced, buffer, new_momentum, staged, sems)
    turn(reduced, turned)
    for item in copies:
        item.wait()


def rest_of_kernel(inverse, a20, a21, b1, b3, b20, b21, before, reduced, squares):
    for layer, (own, other) in enumerate(((a20, b20), (a21, b21))):
        sources = [own[...], b1[layer], b3[layer], other[...]]
        total = before[layer] + reduce_layer(wide_left(inverse[layer]), sources, reduced, layer)
        squares[layer] = jnp.broadcast_to(jnp.sum(total.T, axis=0, keepdims=True), (8, R))


def momentum_kernel(ids, left, rest, buffer, begun, new_momentum, turned, staged, sems):
    del begun
    copies = []
    for layer in range(LAYERS):
        copies += update_momentum(ids, layer, REST, left[layer], rest, buffer, new_momentum, staged, sems)
    turn(rest, turned)
    for item in copies:
        item.wait()


def weight_kernel(
    ids, left, early, rest, turned, turned_rest, s0, s1, s2, s3, weight, new_weight, new_basis, weight_v, basis_v, sems, basis_sems
):
    copies = []
    for layer in range(LAYERS):
        squares = (s0[layer, 0:1, :] + s1[layer, 0:1, :]) + (s2[layer, 0:1, :] + s3[layer, 0:1, :])
        scale = lax.rsqrt(squares * (1.0 / D) + 1e-06)
        wide = wide_left(left[layer] * (scale * (0.05 * math.sqrt(D / R))))
        for where, source, columned in ((EARLY, early, turned), (REST, rest, turned_rest)):
            for slot, cut in spots(ids, where):
                basis_v[layer, cut, :] = (columned[layer, slot] * scale).astype(BF16)
                index = len(copies) - layer
                change = stacked_dot(wide, source[layer, slot])
                weight_v[index] = (1.0 - 0.05 * 0.1) * weight[layer, :, cut] - change
                copies.append(pltpu.make_async_copy(weight_v.at[index], new_weight.at[layer, :, cut], sems.at[index]))
                copies[-1].start()
        copies.append(pltpu.make_async_copy(basis_v.at[layer], new_basis.at[layer], basis_sems.at[layer]))
        copies[-1].start()
    for item in copies:
        item.wait()


def place(z, x, core):
    return (z * 4 + x) * 2 + core


def move_core(a):
    return lax.ppermute(a, "fsdp", [(i, i ^ 1) for i in range(64)])


def move_x(a, flip):
    moves = [(place(z, x, c), place(z, x ^ flip, c)) for z in range(8) for x in range(4) for c in range(2)]
    return lax.ppermute(a, "fsdp", moves)


def swap_z(a):
    groups = [[place(z, x, c) for z in range(8)] for x in range(4) for c in range(2)]
    return lax.all_to_all(a, "fsdp", 0, 0, axis_index_groups=groups, tiled=True)


def move_tp(a, flip):
    return lax.ppermute(a, "tp", [(i, i ^ flip) for i in range(4)])


def body(weight, gradient, momentum, right_basis):
    index = lax.axis_index("fsdp")
    core = index % 2
    ids = jnp.stack([core, (index // 2) % 4]).astype(jnp.int32)

    with jax.named_scope("panel"):
        part = call(
            panel_kernel, struct(LAYERS, ROWS, R), [HBM] * 3, (momentum, gradient, right_basis), 300 << 20, 4 << 20,
            scratch=[
                pltpu.VMEM((LAYERS, ROWS, COLS), F32), pltpu.VMEM((LAYERS, ROWS, COLS), BF16),
                pltpu.VMEM((LAYERS, COLS, R), BF16), pltpu.SemaphoreType.DMA((4, 3)),
            ],
            limit=107 << 19,
        )
        parts = [move_tp(part, flip) for flip in (1, 3, 2)]
        buffer = momentum + gradient.astype(F32)
    with jax.named_scope("product"):
        long, short = struct(LAYERS, R + GRAM, PIECE), struct(LAYERS, 3 * R, PIECE)
        panel, lefts, packed, begun = call(
            begin_kernel,
            (
                struct(LAYERS, ROWS, R), struct(LAYERS, 2 * R, 2 * R, dtype=BF16), struct(LAYERS, R // 2, PIECE),
                long,
            ),
            [SM] + [VM] * 5,
            (ids, part, *parts, buffer), 300 << 20, 3 << 20,
        )
        begun_own = call(
            begin_own_kernel, long, [SM] + [VM] * 3, (ids, lefts, packed, buffer), 300 << 20, 2 << 20
        )
        begun = move_core(begun)
        sends = [begun_own[layer] + begun[layer] for layer in range(LAYERS)]
        rest, rest_own = [
            call(
                lambda *refs, flip=flip: rest_kernel(flip, *refs), short, [SM] + [VM] * 2,
                (ids, lefts, buffer), 300 << 20, 2 << 20,
            )
            for flip in (True, False)
        ]
        rest = move_core(rest)
    with jax.named_scope("scatter"):
        got = [move_x(send, flip) for send, flip in zip(sends, FIRST)]
        gram = jnp.stack([send[R:] + more[R:] for send, more in zip(sends, got)])
        rest = rest_own + rest
        own, to1, to3 = rest[:, 0:R], rest[:, R : 2 * R], rest[:, 2 * R :]
        to1 = jnp.concatenate([to1[0], to1[1] + got[1][0:R], gram[1]])
        to3 = jnp.concatenate([to3[0] + got[0][0:R], to3[1], gram[0]])
        chunks = call(sum_x_kernel, struct(8, CHUNK, PIECE), [VM] * 4, (own, move_x(to1, 1), move_x(to3, 3), gram))
        chunks = swap_z(chunks)
    with jax.named_scope("gather"):
        chunks = swap_z(call(sum_z_kernel, struct(8, CHUNK, PIECE), [VM], (chunks,)))
        whole, gram = call(spread_kernel, (struct(LAYERS, R, PIECE), struct(LAYERS, GRAM, PIECE)), [VM], (chunks,))
        group = [whole, move_x(whole, 1), move_x(whole, 3)]
        inverse = call(
            factor_kernel, struct(LAYERS, R, R), [SM] + [VM] * 2, (ids, gram, move_core(gram)), 8 << 30,
            scratch=[pltpu.VMEM((LAYERS, R, R), F32)],
        )
        inverse, *group[1:] = lax.optimization_barrier((inverse, *group[1:]))
        last = [move_x(group[2][0], 1), move_x(group[1][1], 3)]
        moved = struct(LAYERS, ROWS, COLS)

        def staging(count):
            return [pltpu.VMEM((LAYERS, count, ROWS, PIECE), F32), pltpu.SemaphoreType.DMA((LAYERS, count))]

        four, four_turned = struct(LAYERS, 4, 2 * R, PIECE, dtype=BF16), struct(LAYERS, 4, PIECE, R)
        other = move_core(whole)
        left, early, total, turned, new_momentum = call(
            early_kernel, (struct(LAYERS, ROWS, R), four, struct(LAYERS, R, R), four_turned, moved), [SM] + [VM] * 7,
            (ids, panel, inverse, *group, other, buffer), 3 << 30, 3 << 20, scratch=staging(4),
            out_specs=(VM, VM, VM, VM, HBM),
        )
        total, *last = lax.optimization_barrier((total, *last))
        total, *group[1:] = lax.optimization_barrier((total, *group[1:]))
        others = [move_core(item) for item in (*group[1:], *last)]
    with jax.named_scope("update"):
        rest, squares = call(
            rest_of_kernel, (four, struct(LAYERS, 8, R)), [VM] * 8,
            (inverse, *last, *others, total), 1 << 30,
        )
        shares = [squares] + [move_tp(squares, flip) for flip in (1, 2, 3)]
        new_momentum, turned_rest = call(
            momentum_kernel, (moved, four_turned), [SM] + [VM] * 3 + [HBM],
            (ids, left, rest, buffer, new_momentum), 3 << 30, 2 << 20,
            scratch=staging(4), out_specs=(HBM, VM), aliases={4: 0},
        )
        new_weight, new_basis = call(
            weight_kernel, (moved, struct(LAYERS, COLS, R, dtype=BF16)), [SM] + [VM] * 10,
            (ids, left, early, rest, turned, turned_rest, *shares, weight), 800 << 20, 6 << 20,
            scratch=[
                pltpu.VMEM((16, ROWS, PIECE), F32), pltpu.VMEM((LAYERS, COLS, R), BF16),
                pltpu.SemaphoreType.DMA((16,)), pltpu.SemaphoreType.DMA((LAYERS,)),
            ],
            out_specs=(HBM,) * 2,
        )
    return (new_weight, new_momentum, new_basis)


def solution(mesh):
    return jax.shard_map(
        body,
        mesh=mesh,
        in_specs=(
            P(None, "fsdp", "tp"),
            P(None, "fsdp", "tp"),
            P(None, "fsdp", "tp"),
            P(None, "tp", None),
        ),
        out_specs=(P(None, "fsdp", "tp"), P(None, "fsdp", "tp"), P(None, "tp", None)),
        check_vma=False,
    )
```

```python
import math

import jax
import jax.numpy as jnp
from jax import lax
from jax.experimental import pallas as pl
from jax.experimental.pallas import tpu as pltpu
from jax.sharding import PartitionSpec as P

D = 8192
R = 128
LAYERS = 2
ROWS = 128
COLS = 2048
PIECE = 256
BAND = 16
GRAM = 32
CHUNK = 2 * BAND + 8
BLOCK = 8

HIGHEST = lax.Precision.HIGHEST
F32 = jnp.float32
BF16 = jnp.bfloat16

VM = pl.BlockSpec(memory_space=pltpu.VMEM)
SM = pl.BlockSpec(memory_space=pltpu.SMEM)
ANY = pl.BlockSpec(memory_space=pl.ANY)
HBM = pl.BlockSpec(memory_space=pltpu.HBM)


def struct(*shape, dtype=F32):
    return jax.ShapeDtypeStruct(shape, dtype)


def call(kernel, outs, ins, args, flops=1 << 20, nbytes=1 << 20, scratch=(), out_specs=None, limit=16 << 20, aliases=None):
    return pl.pallas_call(
        kernel,
        out_shape=outs,
        in_specs=ins,
        out_specs=out_specs or jax.tree.map(lambda _: VM, outs),
        scratch_shapes=list(scratch),
        input_output_aliases=aliases or {},
        compiler_params=pltpu.CompilerParams(vmem_limit_bytes=limit),
        cost_estimate=pl.CostEstimate(flops=flops, bytes_accessed=nbytes, transcendentals=0),
    )(*args)


def split2(a):
    high = a.astype(BF16)
    return high, (a - high.astype(F32)).astype(BF16)


def split3(a):
    high = a.astype(BF16)
    rest = a - high.astype(F32)
    mid = rest.astype(BF16)
    return high, mid, (rest - mid.astype(F32)).astype(BF16)


def dot(a, b, dims):
    return lax.dot_general(a, b, (dims, ((), ())), preferred_element_type=F32)


def dot_x3(a, b, dims):
    ah, al = split2(a)
    bh, bl = split2(b)
    return dot(ah, bh, dims) + (dot(ah, bl, dims) + dot(al, bh, dims))


def panel_kernel(momentum, gradient, right, out, mom_v, grad_v, right_v, sems):
    pieces = 2
    width = COLS // pieces
    copies = []
    for layer in range(LAYERS):
        for piece in range(pieces):
            cut = slice(piece * width, (piece + 1) * width)
            slot = len(copies)
            group = [
                pltpu.make_async_copy(momentum.at[layer, :, cut], mom_v.at[layer, :, cut], sems.at[slot, 0]),
                pltpu.make_async_copy(gradient.at[layer, :, cut], grad_v.at[layer, :, cut], sems.at[slot, 1]),
                pltpu.make_async_copy(right.at[layer, cut, :], right_v.at[layer, cut, :], sems.at[slot, 2]),
            ]
            for item in group:
                item.start()
            copies.append(group)
    for layer in range(LAYERS):
        total = jnp.zeros((ROWS, R), F32)
        for piece in range(pieces):
            for item in copies[layer * pieces + piece]:
                item.wait()
            cut = slice(piece * width, (piece + 1) * width)
            buffer = mom_v[layer, :, cut] + grad_v[layer, :, cut].astype(F32)
            factor = right_v[layer, cut, :]
            both = dot(jnp.concatenate(split2(buffer), axis=0), factor, ((1,), (0,)))
            total += both[0:ROWS] + both[ROWS:]
        out[layer] = total


def chunk_of(ids, core, rel):
    return core * 4 + lax.bitwise_xor(ids[1], rel)


def columns(ids, core, rel):
    return pl.ds(pl.multiple_of(chunk_of(ids, core, rel) * PIECE, PIECE), PIECE)


FIRST = (1, 3)
FAR, REST_OF_X = (2,), (0, 1, 3)


def gram_of(panel):
    high, mid, low = split3(panel)
    left = jnp.concatenate([high, mid, high, mid, low, high], axis=0)
    right = jnp.concatenate([high, high, mid, mid, high, low], axis=0)
    return dot(left, right, ((0,), (0,)))


def product(ids, core, rels, lefts, buffer, out):
    for layer in range(LAYERS):
        left = lefts[layer]
        for slot, rel in enumerate(rels):
            out[layer, slot * R : (slot + 1) * R] = wide_dot(left, buffer[layer, :, columns(ids, core, rel)])


def begin_kernel(ids, p0, p1, p2, p3, buffer, panel, lefts, packed, out):
    for layer in range(LAYERS):
        whole = (p0[layer] + p1[layer]) + (p2[layer] + p3[layer])
        panel[layer] = whole
        lefts[layer] = wide_left(whole.T)
        gram = gram_of(whole)
        packed[layer, :, 0:R] = gram[0 : R // 2]
        packed[layer, :, R:] = gram[R // 2 :]
        out[layer, R:] = packed[layer, pl.ds(pl.multiple_of((1 - ids[0]) * GRAM, GRAM), GRAM)]
    product(ids, 1 - ids[0], FAR, lefts, buffer, out)


def begin_own_kernel(ids, lefts, packed, buffer, out):
    for layer in range(LAYERS):
        out[layer, R:] = packed[layer, pl.ds(pl.multiple_of(ids[0] * GRAM, GRAM), GRAM)]
    product(ids, ids[0], FAR, lefts, buffer, out)


def rest_kernel(flip, ids, lefts, buffer, out):
    product(ids, 1 - ids[0] if flip else ids[0], REST_OF_X, lefts, buffer, out)


def sum_x_kernel(own, got1, got3, gram, out):
    for layer, last in enumerate((got3, got1)):
        rows = slice(layer * R, (layer + 1) * R)
        total = own[layer] + (got1[rows] + got3[rows])
        grams = gram[layer] + last[2 * R :]
        for z in range(8):
            out[z, layer * BAND : (layer + 1) * BAND] = total[z * BAND : (z + 1) * BAND]
            start = 2 * BAND + 4 * layer
            out[z, start : start + 4] = grams[4 * z : 4 * z + 4]


def sum_z_kernel(got, out):
    total = (got[0] + got[1]) + (got[2] + got[3]) + ((got[4] + got[5]) + (got[6] + got[7]))
    for z in range(8):
        out[z] = total


def spread_kernel(got, out, gram):
    for layer in range(LAYERS):
        for z in range(8):
            out[layer, z * BAND : (z + 1) * BAND] = got[z, layer * BAND : (layer + 1) * BAND]
            start = 2 * BAND + 4 * layer
            gram[layer, 4 * z : 4 * z + 4] = got[z, start : start + 4]


def factor_kernel(ids, own, other, out, work):
    core = ids[0]
    for index, gram in ((core, own), (1 - core, other)):
        for half in range(2):
            rows = pl.ds(pl.multiple_of(index * GRAM + half * (R // 2), GRAM), GRAM)
            for layer in range(LAYERS):
                work[layer, rows, :] = gram[layer, :, half * R : (half + 1) * R]
    factor(work, out, 0, R)


def factor(work, out, begin, end):
    lane = lax.broadcasted_iota(jnp.int32, (1, R), 1)
    for base in range(begin, end, BLOCK):
        after = base + BLOCK
        inside = (lane >= base) & (lane < after)
        rows = [
            jnp.concatenate([work[layer, base + i : base + i + 1, :] for layer in range(LAYERS)], axis=0)
            for i in range(BLOCK)
        ]
        square = [
            [jnp.broadcast_to(rows[i][:, base + j : base + j + 1], (LAYERS, R)) for j in range(i + 1)]
            for i in range(BLOCK)
        ]
        rows = [jnp.where(inside, jnp.where(lane == base + i, 1.0, 0.0), rows[i]) for i in range(BLOCK)]
        for j in range(BLOCK):
            inverse = lax.rsqrt(square[j][j])
            rows[j] = rows[j] * inverse
            for i in range(j + 1, BLOCK):
                square[i][j] = square[i][j] * inverse
            for i in range(j + 1, BLOCK):
                for k in range(j + 1, i + 1):
                    square[i][k] = square[i][k] - square[i][j] * square[k][j]
                rows[i] = rows[i] - square[i][j] * rows[j]
        for layer in range(LAYERS):
            done = jnp.concatenate([row[layer : layer + 1] for row in rows], axis=0)
            out[layer, base:after, :] = jnp.where(lane < after, done, 0.0)
            if after < R:
                high, mid, low = split3(done)
                left = jnp.concatenate([high, mid, high, mid, low, high], axis=0)
                right = jnp.concatenate([high, high, mid, mid, high, low], axis=0)
                change = dot(left, right, ((0,), (0,)))
                work[layer, after:, :] = jnp.where(inside, 0.0, work[layer, after:, :]) - change[after:, :]


def wide_left(a):
    high, low = split2(a)
    top = jnp.concatenate([high, high], axis=1)
    bottom = jnp.concatenate([low, jnp.zeros_like(low)], axis=1)
    return jnp.concatenate([top, bottom], axis=0)


def stacked(b):
    return jnp.concatenate(split2(b), axis=0)


def stacked_dot(left, b):
    both = dot(left, b, ((1,), (0,)))
    half = both.shape[0] // 2
    return both[0:half] + both[half:]


def wide_dot(left, b):
    return stacked_dot(left, stacked(b))


EARLY = [(0, 0), (0, 1), (0, 3), (1, 0)]
REST = [(0, 2), (1, 1), (1, 3), (1, 2)]


def spots(ids, where):
    return [(slot, columns(ids, 1 - ids[0] if side else ids[0], rel)) for slot, (side, rel) in enumerate(where)]


def reduce_layer(left, sources, reduced, layer):
    total = jnp.zeros((R, R), F32)
    for slot, source in enumerate(sources):
        part = wide_dot(left, source)
        reduced[layer, slot] = stacked(part)
        square = part * part
        total += square[:, 0:R] + square[:, R:]
    return total


def update_momentum(ids, layer, where, basis, reduced, buffer, new_momentum, staged, sems):
    wide = wide_left(basis * 0.05)
    copies = []
    for slot, cut in spots(ids, where):
        staged[layer, slot] = buffer[layer, :, cut] - stacked_dot(wide, reduced[layer, slot])
        copies.append(
            pltpu.make_async_copy(staged.at[layer, slot], new_momentum.at[layer, :, cut], sems.at[layer, slot])
        )
        copies[-1].start()
    return copies


def turn(reduced, turned):
    for layer in range(LAYERS):
        for slot in range(4):
            turned[layer, slot] = (reduced[layer, slot, 0:R].astype(F32) + reduced[layer, slot, R:].astype(F32)).T


def early_kernel(
    ids, panel, inverse, a0, a1, a3, b0, buffer, left, reduced, total, turned, new_momentum, staged, sems
):
    copies = []
    for layer in range(LAYERS):
        sources = [piece[layer] for piece in (a0, a1, a3, b0)]
        total[layer] = reduce_layer(wide_left(inverse[layer]), sources, reduced, layer)
        basis = lax.dot_general(
            panel[layer], inverse[layer], (((1,), (1,)), ((), ())), precision=HIGHEST, preferred_element_type=F32
        )
        left[layer] = basis
        copies += update_momentum(ids, layer, EARLY, basis, reduced, buffer, new_momentum, staged, sems)
    turn(reduced, turned)
    for item in copies:
        item.wait()


def rest_of_kernel(inverse, a20, a21, b1, b3, b20, b21, before, reduced, squares):
    for layer, (own, other) in enumerate(((a20, b20), (a21, b21))):
        sources = [own[...], b1[layer], b3[layer], other[...]]
        total = before[layer] + reduce_layer(wide_left(inverse[layer]), sources, reduced, layer)
        squares[layer] = jnp.broadcast_to(jnp.sum(total.T, axis=0, keepdims=True), (8, R))


def momentum_kernel(ids, left, rest, buffer, begun, new_momentum, turned, staged, sems):
    del begun
    copies = []
    for layer in range(LAYERS):
        copies += update_momentum(ids, layer, REST, left[layer], rest, buffer, new_momentum, staged, sems)
    turn(rest, turned)
    for item in copies:
        item.wait()


def weight_kernel(
    ids, left, early, rest, turned, turned_rest, s0, s1, s2, s3, weight, new_weight, new_basis, weight_v, basis_v, sems, basis_sems
):
    copies = []
    for layer in range(LAYERS):
        squares = (s0[layer, 0:1, :] + s1[layer, 0:1, :]) + (s2[layer, 0:1, :] + s3[layer, 0:1, :])
        scale = lax.rsqrt(squares * (1.0 / D) + 1e-06)
        wide = wide_left(left[layer] * (scale * (0.05 * math.sqrt(D / R))))
        for where, source, columned in ((EARLY, early, turned), (REST, rest, turned_rest)):
            for slot, cut in spots(ids, where):
                basis_v[layer, cut, :] = (columned[layer, slot] * scale).astype(BF16)
                index = len(copies) - layer
                change = stacked_dot(wide, source[layer, slot])
                weight_v[index] = (1.0 - 0.05 * 0.1) * weight[layer, :, cut] - change
                copies.append(pltpu.make_async_copy(weight_v.at[index], new_weight.at[layer, :, cut], sems.at[index]))
                copies[-1].start()
        copies.append(pltpu.make_async_copy(basis_v.at[layer], new_basis.at[layer], basis_sems.at[layer]))
        copies[-1].start()
    for item in copies:
        item.wait()


def place(z, x, core):
    return (z * 4 + x) * 2 + core


def move_core(a):
    return lax.ppermute(a, "fsdp", [(i, i ^ 1) for i in range(64)])


def move_x(a, flip):
    moves = [(place(z, x, c), place(z, x ^ flip, c)) for z in range(8) for x in range(4) for c in range(2)]
    return lax.ppermute(a, "fsdp", moves)


def swap_z(a):
    groups = [[place(z, x, c) for z in range(8)] for x in range(4) for c in range(2)]
    return lax.all_to_all(a, "fsdp", 0, 0, axis_index_groups=groups, tiled=True)


def move_tp(a, flip):
    return lax.ppermute(a, "tp", [(i, i ^ flip) for i in range(4)])


def body(weight, gradient, momentum, right_basis):
    index = lax.axis_index("fsdp")
    core = index % 2
    ids = jnp.stack([core, (index // 2) % 4]).astype(jnp.int32)

    with jax.named_scope("panel"):
        part = call(
            panel_kernel, struct(LAYERS, ROWS, R), [HBM] * 3, (momentum, gradient, right_basis), 300 << 20, 4 << 20,
            scratch=[
                pltpu.VMEM((LAYERS, ROWS, COLS), F32), pltpu.VMEM((LAYERS, ROWS, COLS), BF16),
                pltpu.VMEM((LAYERS, COLS, R), BF16), pltpu.SemaphoreType.DMA((4, 3)),
            ],
            limit=107 << 19,
        )
        parts = [move_tp(part, flip) for flip in (1, 3, 2)]
        buffer = momentum + gradient.astype(F32)
    with jax.named_scope("product"):
        long, short = struct(LAYERS, R + GRAM, PIECE), struct(LAYERS, 3 * R, PIECE)
        panel, lefts, packed, begun = call(
            begin_kernel,
            (
                struct(LAYERS, ROWS, R), struct(LAYERS, 2 * R, 2 * R, dtype=BF16), struct(LAYERS, R // 2, PIECE),
                long,
            ),
            [SM] + [VM] * 5,
            (ids, part, *parts, buffer), 300 << 20, 3 << 20,
        )
        begun_own = call(
            begin_own_kernel, long, [SM] + [VM] * 3, (ids, lefts, packed, buffer), 300 << 20, 2 << 20
        )
        begun = move_core(begun)
        sends = [begun_own[layer] + begun[layer] for layer in range(LAYERS)]
        rest, rest_own = [
            call(
                lambda *refs, flip=flip: rest_kernel(flip, *refs), short, [SM] + [VM] * 2,
                (ids, lefts, buffer), 300 << 20, 2 << 20,
            )
            for flip in (True, False)
        ]
        rest = move_core(rest)
    with jax.named_scope("scatter"):
        got = [move_x(send, flip) for send, flip in zip(sends, FIRST)]
        gram = jnp.stack([send[R:] + more[R:] for send, more in zip(sends, got)])
        rest = rest_own + rest
        own, to1, to3 = rest[:, 0:R], rest[:, R : 2 * R], rest[:, 2 * R :]
        to1 = jnp.concatenate([to1[0], to1[1] + got[1][0:R], gram[1]])
        to3 = jnp.concatenate([to3[0] + got[0][0:R], to3[1], gram[0]])
        chunks = call(sum_x_kernel, struct(8, CHUNK, PIECE), [VM] * 4, (own, move_x(to1, 1), move_x(to3, 3), gram))
        chunks = swap_z(chunks)
    with jax.named_scope("gather"):
        chunks = swap_z(call(sum_z_kernel, struct(8, CHUNK, PIECE), [VM], (chunks,)))
        whole, gram = call(spread_kernel, (struct(LAYERS, R, PIECE), struct(LAYERS, GRAM, PIECE)), [VM], (chunks,))
        group = [whole, move_x(whole, 1), move_x(whole, 3)]
        inverse = call(
            factor_kernel, struct(LAYERS, R, R), [SM] + [VM] * 2, (ids, gram, move_core(gram)), 8 << 30,
            scratch=[pltpu.VMEM((LAYERS, R, R), F32)],
        )
        inverse, *group[1:] = lax.optimization_barrier((inverse, *group[1:]))
        last = [move_x(group[2][0], 1), move_x(group[1][1], 3)]
        moved = struct(LAYERS, ROWS, COLS)

        def staging(count):
            return [pltpu.VMEM((LAYERS, count, ROWS, PIECE), F32), pltpu.SemaphoreType.DMA((LAYERS, count))]

        four, four_turned = struct(LAYERS, 4, 2 * R, PIECE, dtype=BF16), struct(LAYERS, 4, PIECE, R)
        other = move_core(whole)
        left, early, total, turned, new_momentum = call(
            early_kernel, (struct(LAYERS, ROWS, R), four, struct(LAYERS, R, R), four_turned, moved), [SM] + [VM] * 7,
            (ids, panel, inverse, *group, other, buffer), 3 << 30, 3 << 20, scratch=staging(4),
            out_specs=(VM, VM, VM, VM, HBM),
        )
        total, *last = lax.optimization_barrier((total, *last))
        total, *group[1:] = lax.optimization_barrier((total, *group[1:]))
        others = [move_core(item) for item in (*group[1:], *last)]
    with jax.named_scope("update"):
        rest, squares = call(
            rest_of_kernel, (four, struct(LAYERS, 8, R)), [VM] * 8,
            (inverse, *last, *others, total), 1 << 30,
        )
        shares = [squares] + [move_tp(squares, flip) for flip in (1, 2, 3)]
        new_momentum, turned_rest = call(
            momentum_kernel, (moved, four_turned), [SM] + [VM] * 3 + [HBM],
            (ids, left, rest, buffer, new_momentum), 3 << 30, 2 << 20,
            scratch=staging(4), out_specs=(HBM, VM), aliases={4: 0},
        )
        new_weight, new_basis = call(
            weight_kernel, (moved, struct(LAYERS, COLS, R, dtype=BF16)), [SM] + [VM] * 10,
            (ids, left, early, rest, turned, turned_rest, *shares, weight), 800 << 20, 6 << 20,
            scratch=[
                pltpu.VMEM((16, ROWS, PIECE), F32), pltpu.VMEM((LAYERS, COLS, R), BF16),
                pltpu.SemaphoreType.DMA((16,)), pltpu.SemaphoreType.DMA((LAYERS,)),
            ],
            out_specs=(HBM,) * 2,
        )
    return (new_weight, new_momentum, new_basis)


def solution(mesh):
    return jax.shard_map(
        body,
        mesh=mesh,
        in_specs=(
            P(None, "fsdp", "tp"),
            P(None, "fsdp", "tp"),
            P(None, "fsdp", "tp"),
            P(None, "tp", None),
        ),
        out_specs=(P(None, "fsdp", "tp"), P(None, "fsdp", "tp"), P(None, "tp", None)),
        check_vma=False,
    )
```
